128 devices in a mesh: dp: 16 (over y, x), row: 2 (over core), col: 4 (over z).
Axes of the slice: x: 4, y: 4, z: 4, core: 2. Of those that a mesh axis runs over, the one named last changes fastest.
Arguments:
- tokens: bfloat16 [16384, 8192], P(('dp', 'row'), 'col'), may hold values from -2200 to 2200, as said below
- gain: bfloat16 [8192], P('col'), may hold values from 0.5 to 1.5
- weight: bfloat16 [8192, 2048], P('col', 'row'), may hold values from -0.0625 to 0.0625
- d_out: bfloat16 [16384, 2048], P(('dp', 'col'), 'row'), may hold values from -6 to 6
- d_residual: bfloat16 [16384, 8192], P(('dp', 'row'), 'col'), may hold values from -1.5 to 1.5
Outputs:
- d_tokens: bfloat16 [16384, 8192], P(('dp', 'row'), 'col')
- d_weight: bfloat16 [8192, 2048], P(('col', 'dp'), 'row')
- d_gain: float32 [8192], P('col')
- d_log_scale: float32 [16384], P(('dp', 'row'))
The draws below stay inside these ranges and needn't reach their ends.
Inputs may be any that keep to these rules, and one draw needn't show every extreme that they name: `tokens`: finite activations whose rows and features have differing scales.
All inputs are finite; a program needn't handle non-finite values.
Results may differ from the reference program's by a relative error of at most 0.017.
Values may be sent and summed in bfloat16 or wider, within the bound.
A program may use at most 64 MiB of HBM per device.

```python
import math
import jax
import jax.numpy as jnp
from jax import lax

D = 8192
TOK_DEV = 512
QKV = 2048
TOKENS = 16384
N_DP = 16
N_ROW = 2


def draw_tokens(key, part):
    key = jax.random.fold_in(key, 7)
    keys = jax.random.split(key, 3)
    row_scale = jnp.exp(jax.random.uniform(keys[1], (TOKENS, 1), jnp.float32) * math.log(10.0))
    col_scale = jnp.exp(jax.random.uniform(keys[2], (1, D), jnp.float32) * math.log(10.0))
    position = jnp.arange(D, dtype=jnp.float32)[None, :] / (D - 1)
    base = jnp.clip(jax.random.normal(keys[0], (TOKENS, D), jnp.float32), -4.0, 4.0)
    ramp = 1.0 + 2.0 * position
    return (base * row_scale * col_scale * ramp).astype(jnp.bfloat16)


def levels(own_key, extent, cuts, low, high):
    loudness, own = 1.0, jax.random.fold_in(own_key, 6)
    for dim, shards_of in cuts:
        draws = jnp.exp(jax.random.uniform(jax.random.fold_in(own, dim), (shards_of,), jnp.float32, low / len(cuts), high / len(cuts)))
        loudness = loudness * jnp.repeat(draws, extent[dim] // shards_of).reshape([-1 if axis == dim else 1 for axis in range(len(extent))])
    return loudness


def centred(key, dims, scale, most, pieces=(), kind=jnp.bfloat16):
    result = jax.random.normal(key, dims, jnp.float32) * scale
    if len(pieces) > 0:
        result = levels(key, dims, pieces, -0.22, 0.18) * result
    return jnp.clip(result, min=-most, max=most).astype(kind)


def setup_inputs(seed: int = 0) -> dict:
    seeds = jax.random.split(jax.random.key(seed), 6)
    tokens = draw_tokens(jax.random.fold_in(seeds[5], 71), 0)
    gain = jnp.clip(1.0 + 0.1 * jax.random.normal(seeds[1], (D,), jnp.float32), 0.5, 1.5).astype(jnp.bfloat16)
    weight = centred(seeds[2], (D, QKV), D ** -0.5, 0.0625, ((0, 4), (1, 2)))
    d_out = centred(seeds[3], (TOKENS, QKV), 1.0, 6.0, ((0, 64), (1, 2)))
    d_residual = centred(seeds[4], (TOKENS, D), 0.1, 1.5, ((0, 32), (1, 4)))
    return {"tokens": tokens, "gain": gain, "weight": weight, "d_out": d_out, "d_residual": d_residual}


def reference(tokens, gain, weight, d_out, d_residual):
    tok_float = tokens.astype(jnp.float32)
    gain_float = gain.astype(jnp.float32)
    square_sum = lax.optimization_barrier(jnp.sum(tok_float * tok_float, axis=1, keepdims=True))
    inv_rms = lax.rsqrt(square_sum / D + 1e-05)
    normed = (tok_float * inv_rms * gain_float).astype(jnp.bfloat16)
    d_normed = jnp.dot(d_out, weight.T, preferred_element_type=jnp.float32)
    replica_rows = TOK_DEV * N_ROW
    normed_blocks = normed.reshape(N_DP, replica_rows, D)
    grad_blocks = d_out.reshape(N_DP, replica_rows, QKV)

    def add_replica(carry, pair):
        product = jnp.dot(pair[0].T, pair[1], preferred_element_type=jnp.float32)
        rounded = lax.optimization_barrier(product.astype(jnp.bfloat16))
        return (carry + rounded.astype(jnp.float32), None)
    summed, unused = lax.scan(add_replica, jnp.zeros((D, QKV), jnp.float32), (normed_blocks, grad_blocks))
    scale = float(TOKENS) ** (-0.5)
    d_weight = (summed * scale).astype(jnp.bfloat16)
    d_gain = lax.optimization_barrier(jnp.sum(d_normed * tok_float * inv_rms, axis=0)) * scale
    scaled = d_normed * gain_float
    inner = lax.optimization_barrier(jnp.sum(scaled * tok_float, axis=1, keepdims=True))
    d_log_scale = (inner * inv_rms)[:, 0] * float(D) ** (-0.5)
    d_tokens = d_residual.astype(jnp.float32) + inv_rms * scaled - tok_float * (inv_rms * inv_rms * inv_rms) * inner / D
    return (d_tokens.astype(jnp.bfloat16), d_weight, d_gain, d_log_scale)
```

```python
import jax
import jax.numpy as jnp
from jax import lax
from jax.experimental import pallas as pl
from jax.experimental.pallas import tpu as pltpu
from jax.sharding import PartitionSpec as P

MESH = pl.DeviceIdType.MESH
BF16, F32 = jnp.bfloat16, jnp.float32
D = 8192
TOKENS = 16384
ROWS = 512
FEATS = 2048
COLS = 1024
QUARTER = 256
SIDE = 4
CHUNKS = ((0, 128), (128, 128), (256, 256), (512, 256), (768, 128), (896, 128))
N = len(CHUNKS)
PARTS = ((0, 512), (512, 512))


def dot(a, b, dims):
    return lax.dot_general(a, b, ((dims[:1], dims[1:]), ((), ())), preferred_element_type=F32)


def kernel(*refs):
    it = iter(refs)
    tok_hbm, gain_ref, w_hbm, dout_hbm, dres_hbm = [next(it) for _ in range(5)]
    dtok_hbm, dw_hbm, dgain_ref, dlog_ref = [next(it) for _ in range(4)]
    tok, tok_peer, grads, other, w, w_peer, dn, dres, scaled_t = [next(it) for _ in range(9)]
    lanes, sq, inv_row, inv_col, coef_col, inner_buf, dg_acc = [next(it) for _ in range(7)]
    dg_core, dg_x, dg_y, dw_t, dw_out = [next(it) for _ in range(5)]
    part, got1a, got1b, mid, got2a, got2b = [[next(it) for _ in range(N)] for _ in range(6)]
    local_sem, ag_s, ag_r, tp_s, tp_r, wp_s, wp_r, ot_s, ot_r = [next(it) for _ in range(9)]
    sq_s, sq_r, in_s, in_r, dgc_s, dgc_r, dgx_s, dgx_r, dgy_s, dgy_r = [next(it) for _ in range(10)]
    rs_s, rs_r, out_sem = [next(it) for _ in range(3)]

    dp, r, z = lax.axis_index("dp"), lax.axis_index("row"), lax.axis_index("col")
    y, x = dp // SIDE, dp % SIDE

    def dev(dy=0, dx=0, dr=0, dz=0):
        return ((y + dy) % SIDE * SIDE + (x + dx) % SIDE, (r + dr) % 2, (z + dz) % SIDE)

    sent = []

    def send(src, dst, ss, rs, to):
        c = pltpu.make_async_remote_copy(
            src_ref=src, dst_ref=dst, send_sem=ss, recv_sem=rs, device_id=to, device_id_type=MESH
        )
        c.start()
        sent.append(c)

    def arrived(dst, ss, rs):
        pltpu.make_async_remote_copy(
            src_ref=dst, dst_ref=dst, send_sem=ss, recv_sem=rs, device_id=dev(dr=1), device_id_type=MESH
        ).wait_recv()

    def load(src, dst, i):
        c = pltpu.make_async_copy(src, dst, local_sem.at[i])
        c.start()
        return c

    def slot(q):
        return pl.ds(pl.multiple_of((q + 2 * r) % SIDE * QUARTER, QUARTER), QUARTER)

    def half_slot(q, half):
        return pl.ds(pl.multiple_of((q + 2 * r) % SIDE * QUARTER + half * 128, 128), 128)

    tok_load = load(tok_hbm, tok, 0)
    own_load = load(dout_hbm, grads.at[slot(z)], 1)
    w_load = load(w_hbm, w, 2)
    res_load = load(dres_hbm, dres, 3)

    partners = [dev(dr=1)]
    partners += [dev(dz=d) for d in (1, 2, 3)] + [dev(dr=1, dz=d) for d in (1, 2, 3)]
    partners += [dev(dx=d) for d in (1, 2, 3)] + [dev(dy=d) for d in (1, 2, 3)]
    barrier = pltpu.get_barrier_semaphore()
    for partner in partners:
        pl.semaphore_signal(barrier, inc=1, device_id=partner, device_id_type=MESH)

    tok_load.wait()

    @pl.loop(0, ROWS // 16)
    def _(i):
        rows = pl.ds(pl.multiple_of(i * 16, 16), 16)
        acc = jnp.zeros((16, 128), F32)
        for j in range(FEATS // 128):
            t = tok[rows, pl.ds(j * 128, 128)].astype(F32)
            acc += t * t
        lanes[rows, :] = acc

    def lane_sums():
        total = jnp.sum(lanes[...].T, axis=0, keepdims=True)
        return jnp.broadcast_to(total, (8, ROWS))

    sq[0, z] = lane_sums()
    pl.semaphore_wait(barrier, len(partners))

    def columns(k):
        return pl.ds(CHUNKS[k][0], CHUNKS[k][1])

    def gather_send(k):
        src = dout_hbm.at[:, columns(k)]
        dst = grads.at[slot(z), columns(k)]
        send(src, dst, ag_s.at[k, 0], ag_r.at[k, 0], dev(dz=1))
        send(src, dst, ag_s.at[k, 1], ag_r.at[k, 1], dev(dz=3))
        if k == 0:
            send(src, dst, ag_s.at[k, 2], ag_r.at[k, 2], dev(dz=2))

    def gather_relay(k):
        if k == 0:
            return
        low, high = grads.at[half_slot(z + 1, 0), columns(k)], grads.at[half_slot(z + 3, 1), columns(k)]
        arrived(grads.at[slot(z + 3), columns(k)], ag_s.at[k, 0], ag_r.at[k, 0])
        send(high, high, ag_s.at[k, 3], ag_r.at[k, 3], dev(dz=1))
        arrived(grads.at[slot(z + 1), columns(k)], ag_s.at[k, 1], ag_r.at[k, 1])
        send(low, low, ag_s.at[k, 2], ag_r.at[k, 2], dev(dz=3))

    def gather_wait(k):
        if k == 0:
            for j, d in ((0, 3), (1, 1), (2, 2)):
                arrived(grads.at[slot(z + d), columns(k)], ag_s.at[k, j], ag_r.at[k, j])
            own_load.wait()
        else:
            arrived(grads.at[half_slot(z + 2, 0), columns(k)], ag_s.at[k, 2], ag_r.at[k, 2])
            arrived(grads.at[half_slot(z + 2, 1), columns(k)], ag_s.at[k, 3], ag_r.at[k, 3])
        send(
            grads.at[pl.ds(ROWS, ROWS), columns(k)], other.at[:, columns(k)], ot_s.at[k], ot_r.at[k], dev(dr=1)
        )

    send(sq.at[0, z], sq.at[1, z], sq_s.at[0], sq_r.at[1, z], dev(dr=1))
    for d in (1, 2, 3):
        send(sq.at[0, z], sq.at[0, z], sq_s.at[d], sq_r.at[0, z], dev(dz=d))
        send(sq.at[0, z], sq.at[1, z], sq_s.at[3 + d], sq_r.at[1, z], dev(dr=1, dz=d))
    gather_send(0)
    for b in range(SIDE):
        cols = pl.ds(b * 512, 512)
        send(tok_hbm.at[:, cols], tok_peer.at[:, cols], tp_s.at[b], tp_r.at[b], dev(dr=1))
    gather_send(1)
    gather_send(2)
    for b in range(SIDE):
        rows = pl.ds(b * 512, 512)
        send(w_hbm.at[rows], w_peer.at[rows], wp_s.at[b], wp_r.at[b], dev(dr=1))

    for d in (1, 2, 3):
        q = (z + d) % SIDE
        arrived(sq.at[0, q], sq_s.at[0], sq_r.at[0, q])
    for q in range(SIDE):
        arrived(sq.at[1, q], sq_s.at[0], sq_r.at[1, q])
    for side in range(2):
        total = sq[side, 0] + sq[side, 1] + sq[side, 2] + sq[side, 3]
        inv_row[:, pl.ds(side * ROWS, ROWS)] = lax.rsqrt(total * (1.0 / D) + 1e-05)

    def as_column(row):
        return jnp.broadcast_to(row[0:1], (128, ROWS)).T

    inv_col[...] = as_column(inv_row[:, 0:ROWS])

    def product(k):
        start, width = CHUNKS[k]
        cq = width // 4
        for s in range(SIDE):
            toks = pl.ds(s * QUARTER, QUARTER)
            g = grads[toks, pl.ds(start, width)].T.astype(F32)
            scaled_t[pl.ds(0, width), toks] = (g * inv_row[0:1, toks]).astype(BF16)

        def block(b):
            feats = pl.ds(b * 512, 512) if isinstance(b, int) else pl.ds(pl.multiple_of(b * 512, 512), 512)
            res = dot(scaled_t[pl.ds(0, width), pl.ds(0, ROWS)], tok[:, feats], (1, 0))
            res += dot(scaled_t[pl.ds(0, width), pl.ds(ROWS, ROWS)], tok_peer[:, feats], (1, 0))
            res = res.astype(BF16)
            for j in range(SIDE):
                for h in range(2):
                    for u in range(2):
                        lo = (2 * h + u) * cq
                        piece = res[lo : lo + cq, j * 128 : j * 128 + 128]
                        if h == 0:
                            part[k][h, u, j, b] = piece
                        else:
                            part[k][h, u, b, j] = piece

        if k == 0:
            for b in range(SIDE):
                cols = pl.ds(b * 512, 512)
                arrived(tok_peer.at[:, cols], tp_s.at[b], tp_r.at[b])
                block(b)
        else:
            pl.loop(0, SIDE)(block)

    def axis(h, stage):
        if (h == 0) == (stage == 0):
            return x, (lambda d: dev(dx=d))
        return y, (lambda d: dev(dy=d))

    def reduce_start(k, stage):
        src, got_a, got_b = (part, got1a, got1b) if stage == 0 else (mid, got2a, got2b)
        for h in range(2):
            m, to = axis(h, stage)
            ss, rs = rs_s.at[k, stage, h], rs_r.at[k, stage, h]
            far, up, down = (m + 2) % SIDE, (m + 1) % SIDE, (m + 3) % SIDE
            send(src[k].at[h, 0, far], got_a[k].at[h, 0], ss.at[0], rs.at[0], to(1))
            send(src[k].at[h, 1, far], got_a[k].at[h, 1], ss.at[1], rs.at[1], to(3))
            send(src[k].at[h, 1, up], got_b[k].at[h, 0, 1], ss.at[2], rs.at[2], to(1))
            send(src[k].at[h, 0, down], got_b[k].at[h, 1, 0], ss.at[3], rs.at[3], to(3))

    def add(a, b):
        return (a.astype(F32) + b.astype(F32)).astype(BF16)

    def reduce_pass(k, stage):
        src, got_a, got_b = (part, got1a, got1b) if stage == 0 else (mid, got2a, got2b)
        for h in range(2):
            m, to = axis(h, stage)
            ss, rs = rs_s.at[k, stage, h], rs_r.at[k, stage, h]
            up, down = (m + 1) % SIDE, (m + 3) % SIDE
            arrived(got_a[k].at[h, 0], ss.at[0], rs.at[0])
            src[k][h, 0, up] = add(src[k][h, 0, up], got_a[k][h, 0])
            send(src[k].at[h, 0, up], got_b[k].at[h, 0, 0], ss.at[4], rs.at[4], to(1))
            arrived(got_a[k].at[h, 1], ss.at[1], rs.at[1])
            src[k][h, 1, down] = add(src[k][h, 1, down], got_a[k][h, 1])
            send(src[k].at[h, 1, down], got_b[k].at[h, 1, 1], ss.at[5], rs.at[5], to(3))

    def reduce_end(k, stage):
        src, got_b = (part, got1b) if stage == 0 else (mid, got2b)
        cq = CHUNKS[k][1] // 4
        for h in range(2):
            m, _ = axis(h, stage)
            ss, rs = rs_s.at[k, stage, h], rs_r.at[k, stage, h]
            arrived(got_b[k].at[h, 0, 1], ss.at[2], rs.at[2])
            arrived(got_b[k].at[h, 1, 0], ss.at[3], rs.at[3])
            arrived(got_b[k].at[h, 0, 0], ss.at[4], rs.at[4])
            arrived(got_b[k].at[h, 1, 1], ss.at[5], rs.at[5])
            for u in range(2):
                total = src[k][h, u, m].astype(F32)
                total += got_b[k][h, 0, u].astype(F32)
                total += got_b[k][h, 1, u].astype(F32)
                if stage == 0:
                    mid[k][h, u] = total.astype(BF16)
                else:
                    dw_t[pl.ds((2 * h + u) * cq, cq), :] = total

    def finish(k):
        start, width = CHUNKS[k]
        own = gain_ref[0:1, pl.ds(pl.multiple_of(dp * 128, 128), 128)].astype(F32) * float(TOKENS) ** (-0.5)
        dw_out[:, pl.ds(start, width)] = (dw_t[pl.ds(0, width), :] * own).T.astype(BF16)

    def normed_grad(p):
        cols = pl.ds(*PARTS[p])
        for k in range(N):
            if PARTS[p][0] <= CHUNKS[k][0] < PARTS[p][0] + PARTS[p][1]:
                arrived(other.at[:, columns(k)], ot_s.at[k], ot_r.at[k])
        if p == 0:
            w_load.wait()
            for b in range(SIDE):
                arrived(w_peer.at[pl.ds(b * 512, 512)], wp_s.at[b], wp_r.at[b])

        @pl.loop(0, SIDE)
        def _(b):
            feats = pl.ds(pl.multiple_of(b * 512, 512), 512)
            res = dot(grads[pl.ds(0, ROWS), cols], w[feats, cols], (1, 1))
            res += dot(other[:, cols], w_peer[feats, cols], (1, 1))
            if p == 0:
                dn[:, feats] = res
            else:
                dn[:, feats] += res

    def inner_start():
        dg_acc[...] = jnp.zeros_like(dg_acc)

        @pl.loop(0, ROWS // 16)
        def _(i):
            rows = pl.ds(pl.multiple_of(i * 16, 16), 16)
            inv = inv_col[rows, :]
            acc = jnp.zeros((16, 128), F32)
            for j in range(FEATS // 128):
                cols = pl.ds(j * 128, 128)
                prod = dn[rows, cols] * tok[rows, cols].astype(F32)
                acc += prod * gain_ref[0:1, cols].astype(F32)
                prod = prod * inv
                dg_acc[:, cols] += prod[0:8] + prod[8:16]
            lanes[rows, :] = acc

        inner_buf[z] = lane_sums()
        for d in (1, 2, 3):
            send(inner_buf.at[z], inner_buf.at[z], in_s.at[d], in_r.at[z], dev(dz=d))
        for j in range(FEATS // 128):
            dg_core[r, pl.ds(j, 1), :] = jnp.sum(dg_acc[:, pl.ds(j * 128, 128)], axis=0, keepdims=True)
        send(dg_core.at[r], dg_core.at[r], dgc_s, dgc_r, dev(dr=1))

    def gain_x():
        arrived(dg_core.at[1 - r], dgc_s, dgc_r)
        dg_x[x] = dg_core[0] + dg_core[1]
        for d in (1, 2, 3):
            send(dg_x.at[x], dg_x.at[x], dgx_s.at[d], dgx_r.at[x], dev(dx=d))

    def gain_y():
        for d in (1, 2, 3):
            q = (x + d) % SIDE
            arrived(dg_x.at[q], dgx_s.at[0], dgx_r.at[q])
        dg_y[y] = dg_x[0] + dg_x[1] + dg_x[2] + dg_x[3]
        for d in (1, 2, 3):
            send(dg_y.at[y], dg_y.at[y], dgy_s.at[d], dgy_r.at[y], dev(dy=d))

    def gain_end():
        for d in (1, 2, 3):
            q = (y + d) % SIDE
            arrived(dg_y.at[q], dgy_s.at[0], dgy_r.at[q])
        dgain_ref[...] = (dg_y[0] + dg_y[1] + dg_y[2] + dg_y[3]) * float(TOKENS) ** (-0.5)

    writes = []

    def write(src, dst, i):
        c = pltpu.make_async_copy(src, dst, out_sem.at[i])
        c.start()
        writes.append(c)

    def tokens_end():
        for d in (1, 2, 3):
            q = (z + d) % SIDE
            arrived(inner_buf.at[q], in_s.at[0], in_r.at[q])
        inner = inner_buf[0] + inner_buf[1] + inner_buf[2] + inner_buf[3]
        inv = inv_row[:, 0:ROWS]
        log_scale = inner * inv * float(D) ** (-0.5)
        for j in range(SIDE):
            dlog_ref[pl.ds(j, 1), :] = log_scale[0:1, j * 128 : j * 128 + 128]
        coef_col[...] = as_column(inv * inv * inv * inner * (1.0 / D))
        res_load.wait()
        for q in range(SIDE):

            @pl.loop(0, 8)
            def _(i):
                rows = pl.ds(pl.multiple_of(q * 128 + i * 16, 16), 16)
                inv_c, coef = inv_col[rows, :], coef_col[rows, :]
                for j in range(FEATS // 128):
                    cols = pl.ds(j * 128, 128)
                    scaled = dn[rows, cols] * gain_ref[0:1, cols].astype(F32)
                    value = dres[rows, cols].astype(F32) + inv_c * scaled
                    dres[rows, cols] = (value - tok[rows, cols].astype(F32) * coef).astype(BF16)

            rows = pl.ds(q * 128, 128)
            write(dres.at[rows], dtok_hbm.at[rows], q)

    for i in range(N + 4):
        if 1 <= i and i + 1 < N:
            gather_relay(i + 1)
            if i + 2 < N:
                gather_send(i + 2)
        if i < N:
            gather_wait(i)
            product(i)
            reduce_start(i, 0)
        if i == 0:
            gather_relay(1)
        if 0 <= i - 1 < N:
            reduce_pass(i - 1, 0)
        if 0 <= i - 2 < N:
            reduce_end(i - 2, 0)
            reduce_start(i - 2, 1)
        if 0 <= i - 3 < N:
            reduce_pass(i - 3, 1)
        if 0 <= i - 4 < N:
            reduce_end(i - 4, 1)
            finish(i - 4)
        if i == 4:
            normed_grad(0)
        if i == N:
            normed_grad(1)
            inner_start()
        if i == N + 1:
            gain_x()
            tokens_end()
        if i == N + 2:
            gain_y()
    write(dw_out, dw_hbm, 4)
    gain_end()
    for c in sent:
        c.wait_send()
    for c in writes:
        c.wait()


def local(tokens, gain, weight, d_out, d_residual):
    vmem, dma = pltpu.VMEM, pltpu.SemaphoreType.DMA
    cqs = [width // 4 for _, width in CHUNKS]
    scratch = [
        vmem((ROWS, FEATS), BF16),
        vmem((ROWS, FEATS), BF16),
        vmem((2 * ROWS, COLS), BF16),
        vmem((ROWS, COLS), BF16),
        vmem((FEATS, COLS), BF16),
        vmem((FEATS, COLS), BF16),
        vmem((ROWS, FEATS), F32),
        vmem((ROWS, FEATS), BF16),
        vmem((256, 2 * ROWS), BF16),
        vmem((ROWS, 128), F32),
        vmem((2, SIDE, 8, ROWS), F32),
        vmem((8, 2 * ROWS), F32),
        vmem((ROWS, 128), F32),
        vmem((ROWS, 128), F32),
        vmem((SIDE, 8, ROWS), F32),
        vmem((8, FEATS), F32),
        vmem((2, 16, 128), F32),
        vmem((SIDE, 16, 128), F32),
        vmem((SIDE, 16, 128), F32),
        vmem((256, 128), F32),
        vmem((128, COLS), BF16),
    ]
    scratch += [vmem((2, 2, SIDE, SIDE, c, 128), BF16) for c in cqs]
    scratch += [vmem((2, 2, SIDE, c, 128), BF16) for c in cqs]
    scratch += [vmem((2, 2, 2, SIDE, c, 128), BF16) for c in cqs]
    scratch += [vmem((2, 2, SIDE, c, 128), BF16) for c in cqs]
    scratch += [vmem((2, 2, c, 128), BF16) for c in cqs]
    scratch += [vmem((2, 2, 2, c, 128), BF16) for c in cqs]
    scratch += [
        dma((4,)),
        dma((N, 4)),
        dma((N, 4)),
        dma((4,)),
        dma((4,)),
        dma((4,)),
        dma((4,)),
        dma((N,)),
        dma((N,)),
        dma((7,)),
        dma((2, SIDE)),
        dma((4,)),
        dma((SIDE,)),
        dma,
        dma,
        dma((4,)),
        dma((SIDE,)),
        dma((4,)),
        dma((SIDE,)),
        dma((N, 2, 2, 6)),
        dma((N, 2, 2, 6)),
        dma((5,)),
    ]
    hbm, in_vmem = pl.BlockSpec(memory_space=pl.ANY), pl.BlockSpec(memory_space=pltpu.VMEM)
    d_tokens, d_weight, d_gain, d_log = pl.pallas_call(
        kernel,
        name="fused",
        out_shape=(
            jax.ShapeDtypeStruct((ROWS, FEATS), BF16),
            jax.ShapeDtypeStruct((128, COLS), BF16),
            jax.ShapeDtypeStruct((16, 128), F32),
            jax.ShapeDtypeStruct((4, 128), F32),
        ),
        in_specs=[hbm, in_vmem, hbm, hbm, hbm],
        out_specs=(hbm, hbm, in_vmem, in_vmem),
        scratch_shapes=scratch,
        compiler_params=pltpu.CompilerParams(
            collective_id=0, has_side_effects=True, vmem_limit_bytes=60 * 2**20
        ),
        cost_estimate=pl.CostEstimate(flops=8 * 2**30, bytes_accessed=12 * 2**20, transcendentals=0),
    )(tokens, gain.reshape(1, FEATS), weight, d_out, d_residual)
    return d_tokens, d_weight, d_gain.reshape(FEATS), d_log.reshape(ROWS)


def solution(mesh):
    in_specs = (
        P(("dp", "row"), "col"),
        P("col"),
        P("col", "row"),
        P(("dp", "col"), "row"),
        P(("dp", "row"), "col"),
    )
    out_specs = (P(("dp", "row"), "col"), P(("col", "dp"), "row"), P("col"), P(("dp", "row")))
    return jax.shard_map(local, mesh=mesh, in_specs=in_specs, out_specs=out_specs, check_vma=False)
```

```python
import jax
import jax.numpy as jnp
from jax import lax
from jax.experimental import pallas as pl
from jax.experimental.pallas import tpu as pltpu
from jax.sharding import PartitionSpec as P

MESH = pl.DeviceIdType.MESH
BF16, F32 = jnp.bfloat16, jnp.float32
D = 8192
TOKENS = 16384
ROWS = 512
FEATS = 2048
COLS = 1024
QUARTER = 256
SIDE = 4
SLABS = 8
CHUNKS = ((0, 1), (1, 1), (2, 2), (4, 2), (6, 1), (7, 1))
N = len(CHUNKS)
STRAIGHT = ((0, 0), (0, 0), (0, 0), (0, 0), (0, 1), (1, 1))
PARTS = (((0, 4), (0, 4)), ((4, 8), (4, 8)))


def dot(a, b, dims):
    return lax.dot_general(a, b, ((dims[:1], dims[1:]), ((), ())), preferred_element_type=F32)


def kernel(*refs):
    it = iter(refs)
    tok_hbm, gain_hbm, w_hbm, dout_hbm, dres_hbm = [next(it) for _ in range(5)]
    dtok_ref, dw_ref, dgain_ref, dlog_ref = [next(it) for _ in range(4)]
    tok, tok_peer, grads, other, w, w_peer, dn, dres, scaled_t = [next(it) for _ in range(9)]
    gain_flat, gain_row, lanes, sq, inv_row, inv_col, coef_col, inner_buf = [next(it) for _ in range(8)]
    dg_acc, dg_a, dg_b, dw_t = [next(it) for _ in range(4)]
    part, got1a, got1b, mid, got2a, got2b = [[next(it) for _ in range(N)] for _ in range(6)]
    local_sem, ag_s, ag_r, tp_s, tp_r, wp_s, wp_r, ot_s, ot_r = [next(it) for _ in range(9)]
    sq_s, sq_r, in_s, in_r, ga_s, ga_r, gb_s, gb_r, rs_s, rs_r = [next(it) for _ in range(10)]

    dp, r, z = lax.axis_index("dp"), lax.axis_index("row"), lax.axis_index("col")
    y, x = dp // SIDE, dp % SIDE

    def dev(dy=0, dx=0, dr=0, dz=0):
        return ((y + dy) % SIDE * SIDE + (x + dx) % SIDE, (r + dr) % 2, (z + dz) % SIDE)

    def send(src, dst, ss, rs, to):
        pltpu.make_async_remote_copy(
            src_ref=src, dst_ref=dst, send_sem=ss, recv_sem=rs, device_id=to, device_id_type=MESH
        ).start()

    def descriptor(ref, sem):
        return pltpu.make_async_remote_copy(
            src_ref=ref, dst_ref=ref, send_sem=sem, recv_sem=sem, device_id=dev(dr=1), device_id_type=MESH
        )

    def arrived(ref, sem):
        descriptor(ref, sem).wait_recv()

    def left(ref, sem):
        descriptor(ref, sem).wait_send()

    def load(src, dst, i):
        c = pltpu.make_async_copy(src, dst, local_sem.at[i])
        c.start()
        return c

    def slot(q):
        return pl.ds(pl.multiple_of((q + 2 * r) % SIDE * QUARTER, QUARTER), QUARTER)

    def half_slot(q, half):
        return pl.ds(pl.multiple_of((q + 2 * r) % SIDE * QUARTER + half * 128, 128), 128)

    def slabs(k):
        return pl.ds(*CHUNKS[k])

    partners = [dev(dr=1)]
    partners += [dev(dz=d) for d in (1, 2, 3)] + [dev(dr=1, dz=d) for d in (1, 2, 3)]
    partners += [dev(dx=d) for d in (1, 2, 3)] + [dev(dr=1, dx=d) for d in (1, 2, 3)]
    partners += [dev(dy=d) for d in (1, 2, 3)]
    barrier = pltpu.get_barrier_semaphore()
    for partner in partners:
        pl.semaphore_signal(barrier, inc=1, device_id=partner, device_id_type=MESH)

    tok_load = load(tok_hbm, tok, 0)
    for c in range(SLABS):
        load(dout_hbm.at[:, pl.ds(c * 128, 128)], grads.at[c, slot(z)], 1)
    gain_load = load(gain_hbm, gain_flat, 2)
    w_load = load(w_hbm, w, 3)
    res_load = load(dres_hbm, dres, 4)

    tok_load.wait()

    @pl.loop(0, ROWS // 16)
    def _(i):
        rows = pl.ds(pl.multiple_of(i * 16, 16), 16)
        acc = jnp.zeros((16, 128), F32)
        for j in range(FEATS // 128):
            t = tok[rows, pl.ds(j * 128, 128)].astype(F32)
            acc += t * t
        lanes[rows, :] = acc

    def lane_sums():
        total = jnp.sum(lanes[...].T, axis=0, keepdims=True)
        return jnp.broadcast_to(total, (8, ROWS))

    own_sq = sq.at[z]
    own_sq[...] = lane_sums()
    own_quarter = grads.at[:, slot(z)]
    pltpu.make_async_copy(own_quarter, own_quarter, local_sem.at[1]).wait()
    pl.semaphore_wait(barrier, len(partners))

    def gather_send(k):
        own = grads.at[slabs(k), slot(z)]
        for d in (1, 3) if k else (1, 3, 2):
            send(own, own, ag_s, ag_r.at[k, 0], dev(dz=d))

    def gather_relay(k):
        if k == 0:
            return
        arrived(grads.at[slabs(k), pl.ds(0, 2 * QUARTER)], ag_r.at[k, 0])
        low, high = grads.at[slabs(k), half_slot(z + 1, 0)], grads.at[slabs(k), half_slot(z + 3, 1)]
        send(low, low, ag_s, ag_r.at[k, 1], dev(dz=3))
        send(high, high, ag_s, ag_r.at[k, 1], dev(dz=1))

    def gather_wait(k):
        if k == 0:
            arrived(grads.at[slabs(k), pl.ds(0, 3 * QUARTER)], ag_r.at[k, 0])
        else:
            arrived(grads.at[slabs(k), pl.ds(0, QUARTER)], ag_r.at[k, 1])
        send(grads.at[slabs(k), pl.ds(ROWS, ROWS)], other.at[slabs(k)], ot_s, ot_r.at[k], dev(dr=1))

    peer_sq = sq.at[SIDE + z]
    for d in (1, 2, 3):
        send(own_sq, own_sq, sq_s, sq_r, dev(dz=d))
        send(own_sq, peer_sq, sq_s, sq_r, dev(dr=1, dz=d))
    send(own_sq, peer_sq, sq_s, sq_r, dev(dr=1))
    gather_send(0)
    for b in range(SIDE):
        cols = pl.ds(b * 512, 512)
        send(tok_hbm.at[:, cols], tok_peer.at[:, cols], tp_s, tp_r.at[b], dev(dr=1))
    gather_send(1)
    gather_send(2)
    send(w_hbm, w_peer, wp_s, wp_r, dev(dr=1))

    gain_load.wait()
    gain_row[...] = gain_flat[...].astype(F32).reshape(1, FEATS)

    arrived(sq.at[pl.ds(0, 7)], sq_r)
    for side in range(2):
        total = sq[4 * side] + sq[4 * side + 1] + sq[4 * side + 2] + sq[4 * side + 3]
        inv_row[:, pl.ds(side * ROWS, ROWS)] = lax.rsqrt(total * (1.0 / D) + 1e-05)

    def as_column(row):
        return jnp.broadcast_to(row[0:1], (128, ROWS)).T

    def product(k):
        first, count = CHUNKS[k]
        width, cq = count * 128, count * 32
        for c in range(count):
            for s in range(SIDE):
                toks = pl.ds(s * QUARTER, QUARTER)
                g = grads[first + c, toks, :].T.astype(F32)
                scaled_t[pl.ds(c * 128, 128), toks] = (g * inv_row[0:1, toks]).astype(BF16)

        def block(b):
            feats = pl.ds(b * 512, 512) if isinstance(b, int) else pl.ds(pl.multiple_of(b * 512, 512), 512)
            res = dot(scaled_t[pl.ds(0, width), pl.ds(0, ROWS)], tok[:, feats], (1, 0))
            res += dot(scaled_t[pl.ds(0, width), pl.ds(ROWS, ROWS)], tok_peer[:, feats], (1, 0))
            res = res.astype(BF16)
            for j in range(SIDE):
                for h in range(2):
                    for u in range(2):
                        lo = (2 * h + u) * cq
                        piece = res[lo : lo + cq, j * 128 : j * 128 + 128]
                        if h == 0:
                            part[k][h, j, u, b] = piece
                        else:
                            part[k][h, b, u, j] = piece

        if k == 0:
            for b in range(SIDE):
                arrived(tok_peer.at[:, pl.ds(b * 512, 512)], tp_r.at[b])
                block(b)
        else:
            pl.loop(0, SIDE)(block)

    def axis(h, stage):
        if (h == 0) == (stage == 0):
            return x, (lambda d: dev(dx=d))
        return y, (lambda d: dev(dy=d))

    def buffers(stage):
        return (part, got1a, got1b) if stage == 0 else (mid, got2a, got2b)

    def reduce_start(k, stage):
        src, got_a, got_b = buffers(stage)
        ss, rs = rs_s.at[k, stage], rs_r.at[k, stage]
        for h in range(2):
            m, to = axis(h, stage)
            far, up, down = (m + 2) % SIDE, (m + 1) % SIDE, (m + 3) % SIDE
            if STRAIGHT[k][stage]:
                send(src[k].at[h, far], got_b[k].at[h, 1], ss, rs.at[0], to(2))
                send(src[k].at[h, up], got_b[k].at[h, 0], ss, rs.at[0], to(1))
                send(src[k].at[h, down], got_b[k].at[h, 2], ss, rs.at[0], to(3))
                continue
            send(src[k].at[h, far, 0], got_a[k].at[h, 0], ss, rs.at[1], to(1))
            send(src[k].at[h, far, 1], got_a[k].at[h, 1], ss, rs.at[1], to(3))
            send(src[k].at[h, up, 1], got_b[k].at[h, 0, 1], ss, rs.at[0], to(1))
            send(src[k].at[h, down, 0], got_b[k].at[h, 1, 0], ss, rs.at[0], to(3))

    def add(a, b):
        return (a.astype(F32) + b.astype(F32)).astype(BF16)

    def reduce_pass(k, stage):
        if STRAIGHT[k][stage]:
            return
        src, got_a, got_b = buffers(stage)
        ss, rs = rs_s.at[k, stage], rs_r.at[k, stage]
        arrived(got_a[k], rs.at[1])
        for h in range(2):
            m, to = axis(h, stage)
            up, down = (m + 1) % SIDE, (m + 3) % SIDE
            src[k][h, up, 0] = add(src[k][h, up, 0], got_a[k][h, 0])
            send(src[k].at[h, up, 0], got_b[k].at[h, 0, 0], ss, rs.at[0], to(1))
            src[k][h, down, 1] = add(src[k][h, down, 1], got_a[k][h, 1])
            send(src[k].at[h, down, 1], got_b[k].at[h, 1, 1], ss, rs.at[0], to(3))

    def reduce_end(k, stage):
        src, _, got_b = buffers(stage)
        cq = CHUNKS[k][1] * 32
        arrived(got_b[k], rs_r.at[k, stage, 0])
        for h in range(2):
            m, _ = axis(h, stage)
            for u in range(2):
                total = src[k][h, m, u].astype(F32)
                for d in range(3 if STRAIGHT[k][stage] else 2):
                    total += got_b[k][h, d, u].astype(F32)
                if stage == 0:
                    for t in range(SIDE):
                        mid[k][h, t, u] = total[t].astype(BF16)
                else:
                    dw_t[pl.ds((2 * h + u) * cq, cq), :] = total

    def finish(k):
        first, count = CHUNKS[k]
        own = gain_row[0:1, pl.ds(pl.multiple_of(dp * 128, 128), 128)] * float(TOKENS) ** (-0.5)
        dw_ref[:, pl.ds(first * 128, count * 128)] = (dw_t[pl.ds(0, count * 128), :] * own).T.astype(BF16)

    def normed_grad(p):
        (own_lo, own_hi), (peer_lo, peer_hi) = PARTS[p]
        for k in range(N):
            if peer_lo <= CHUNKS[k][0] < peer_hi:
                arrived(other.at[slabs(k)], ot_r.at[k])
        if p == 0:
            w_load.wait()
            arrived(w_peer, wp_r)

        @pl.loop(0, SIDE)
        def _(b):
            feats = pl.ds(pl.multiple_of(b * 512, 512), 512)
            own = jnp.concatenate([grads[c, pl.ds(0, ROWS), :] for c in range(own_lo, own_hi)], axis=1)
            res = dot(own, w[feats, pl.ds(own_lo * 128, (own_hi - own_lo) * 128)], (1, 1))
            peer = jnp.concatenate([other[c] for c in range(peer_lo, peer_hi)], axis=1)
            res += dot(peer, w_peer[feats, pl.ds(peer_lo * 128, (peer_hi - peer_lo) * 128)], (1, 1))
            if p == 0:
                dn[:, feats] = res
            else:
                dn[:, feats] += res

    def inner_start():
        inv_col[...] = as_column(inv_row[:, 0:ROWS])
        dg_acc[...] = jnp.zeros_like(dg_acc)

        @pl.loop(0, ROWS // 16)
        def _(i):
            rows = pl.ds(pl.multiple_of(i * 16, 16), 16)
            inv = inv_col[rows, :]
            acc = jnp.zeros((16, 128), F32)
            for j in range(FEATS // 128):
                cols = pl.ds(j * 128, 128)
                prod = dn[rows, cols] * tok[rows, cols].astype(F32)
                acc += prod * gain_row[0:1, cols]
                prod = prod * inv
                dg_acc[:, cols] += prod[0:8] + prod[8:16]
            lanes[rows, :] = acc

        own_inner = inner_buf.at[z]
        own_inner[...] = lane_sums()
        for d in (1, 2, 3):
            send(own_inner, own_inner, in_s, in_r, dev(dz=d))
        own_dg = dg_a.at[r * SIDE + x]
        for j in range(FEATS // 128):
            own_dg[pl.ds(j, 1), :] = jnp.sum(dg_acc[:, pl.ds(j * 128, 128)], axis=0, keepdims=True)
        for d in (1, 2, 3):
            send(own_dg, own_dg, ga_s, ga_r, dev(dx=d))
            send(own_dg, own_dg, ga_s, ga_r, dev(dr=1, dx=d))
        send(own_dg, own_dg, ga_s, ga_r, dev(dr=1))

    def gain_y():
        arrived(dg_a.at[pl.ds(0, 7)], ga_r)
        total = dg_a[0]
        for i in range(1, 8):
            total += dg_a[i]
        own_dg = dg_b.at[y]
        own_dg[...] = total
        for d in (1, 2, 3):
            send(own_dg, own_dg, gb_s, gb_r, dev(dy=d))

    def gain_end():
        arrived(dg_b.at[pl.ds(0, 3)], gb_r)
        dgain_ref[...] = (dg_b[0] + dg_b[1] + dg_b[2] + dg_b[3]) * float(TOKENS) ** (-0.5)

    def tokens_end():
        arrived(inner_buf.at[pl.ds(0, 3)], in_r)
        inner = inner_buf[0] + inner_buf[1] + inner_buf[2] + inner_buf[3]
        inv = inv_row[:, 0:ROWS]
        log_scale = inner * inv * float(D) ** (-0.5)
        for j in range(SIDE):
            dlog_ref[pl.ds(j, 1), :] = log_scale[0:1, j * 128 : j * 128 + 128]
        coef_col[...] = as_column(inv * inv * inv * inner * (1.0 / D))
        res_load.wait()

        @pl.loop(0, ROWS // 16)
        def _(i):
            rows = pl.ds(pl.multiple_of(i * 16, 16), 16)
            inv_c, coef = inv_col[rows, :], coef_col[rows, :]
            for j in range(FEATS // 128):
                cols = pl.ds(j * 128, 128)
                scaled = dn[rows, cols] * gain_row[0:1, cols]
                value = dres[rows, cols].astype(F32) + inv_c * scaled
                dtok_ref[rows, cols] = (value - tok[rows, cols].astype(F32) * coef).astype(BF16)

    def step(k, n):
        if n == 0:
            gather_wait(k)
            product(k)
            reduce_start(k, 0)
        if n == 1:
            reduce_pass(k, 0)
        if n == 2:
            reduce_end(k, 0)
            reduce_start(k, 1)
        if n == 3:
            reduce_pass(k, 1)
        if n == 4:
            reduce_end(k, 1)
            finish(k)

    for i in range(N + 4):
        if 1 <= i and i + 1 < N:
            gather_relay(i + 1)
            if i + 2 < N:
                gather_send(i + 2)
        if i == N:
            normed_grad(1)
            inner_start()
        if i < N:
            step(i, 0)
        if i == 0:
            gather_relay(1)
        for n in range(1, 5):
            if 0 <= i - n < N:
                step(i - n, n)
        if i == 4:
            normed_grad(0)
        if i == N + 1:
            gain_y()
            tokens_end()
    gain_end()
    left(grads.at[pl.ds(0, 6)], ag_s)
    left(tok_peer, tp_s)
    left(w_peer, wp_s)
    left(other, ot_s)
    left(sq.at[pl.ds(0, 7)], sq_s)
    left(inner_buf.at[pl.ds(0, 3)], in_s)
    left(dg_a.at[pl.ds(0, 7)], ga_s)
    left(dg_b.at[pl.ds(0, 3)], gb_s)
    for k in range(N):
        left(part[k].at[:, pl.ds(0, 3)], rs_s.at[k, 0])
        left(mid[k].at[:, pl.ds(0, 3)], rs_s.at[k, 1])


def write_out(dtok, dw, dgain, dlog, dtok_hbm, dw_hbm, dgain_hbm, dlog_hbm, sem):
    pairs = ((dtok, dtok_hbm), (dw, dw_hbm), (dgain, dgain_hbm), (dlog, dlog_hbm))
    copies = [pltpu.make_async_copy(src, dst, sem.at[i]) for i, (src, dst) in enumerate(pairs)]
    for c in copies:
        c.start()
    for c in copies:
        c.wait()


def local(tokens, gain, weight, d_out, d_residual):
    vmem, dma = pltpu.VMEM, pltpu.SemaphoreType.DMA
    cqs = [count * 32 for _, count in CHUNKS]
    scratch = [
        vmem((ROWS, FEATS), BF16),
        vmem((ROWS, FEATS), BF16),
        vmem((SLABS, 2 * ROWS, 128), BF16),
        vmem((SLABS, ROWS, 128), BF16),
        vmem((FEATS, COLS), BF16),
        vmem((FEATS, COLS), BF16),
        vmem((ROWS, FEATS), F32),
        vmem((ROWS, FEATS), BF16),
        vmem((256, 2 * ROWS), BF16),
        vmem((FEATS,), BF16),
        vmem((1, FEATS), F32),
        vmem((ROWS, 128), F32),
        vmem((2 * SIDE, 8, ROWS), F32),
        vmem((8, 2 * ROWS), F32),
        vmem((ROWS, 128), F32),
        vmem((ROWS, 128), F32),
        vmem((SIDE, 8, ROWS), F32),
        vmem((8, FEATS), F32),
        vmem((2 * SIDE, 16, 128), F32),
        vmem((SIDE, 16, 128), F32),
        vmem((256, 128), F32),
    ]
    scratch += [vmem((2, SIDE, 2, SIDE, c, 128), BF16) for c in cqs]
    scratch += [vmem((2, 2, SIDE, c, 128), BF16) for c in cqs]
    scratch += [vmem((2, 2 + s[0], 2, SIDE, c, 128), BF16) for c, s in zip(cqs, STRAIGHT)]
    scratch += [vmem((2, SIDE, 2, c, 128), BF16) for c in cqs]
    scratch += [vmem((2, 2, c, 128), BF16) for c in cqs]
    scratch += [vmem((2, 2 + s[1], 2, c, 128), BF16) for c, s in zip(cqs, STRAIGHT)]
    scratch += [
        dma((5,)),
        dma,
        dma((N, 2)),
        dma,
        dma((SIDE,)),
        dma,
        dma,
        dma,
        dma((N,)),
        dma,
        dma,
        dma,
        dma,
        dma,
        dma,
        dma,
        dma,
        dma((N, 2)),
        dma((N, 2, 2)),
    ]
    hbm, in_vmem = pl.BlockSpec(memory_space=pltpu.HBM), pl.BlockSpec(memory_space=pltpu.VMEM)
    shapes = (((ROWS, FEATS), BF16), ((128, COLS), BF16), ((16, 128), F32), ((4, 128), F32))
    results = pl.pallas_call(
        kernel,
        name="fused",
        out_shape=tuple(pltpu.VMEM(*shape) for shape in shapes),
        in_specs=[hbm] * 5,
        out_specs=(in_vmem,) * 4,
        scratch_shapes=scratch,
        compiler_params=pltpu.CompilerParams(
            collective_id=0, has_side_effects=True, vmem_limit_bytes=48 * 2**20
        ),
        cost_estimate=pl.CostEstimate(flops=8 * 2**30, bytes_accessed=12 * 2**20, transcendentals=0),
    )(*[pltpu.with_memory_space_constraint(a, pltpu.HBM) for a in (tokens, gain, weight, d_out, d_residual)])
    d_tokens, d_weight, d_gain, d_log = pl.pallas_call(
        write_out,
        name="write_out",
        out_shape=tuple(jax.ShapeDtypeStruct(*shape) for shape in shapes),
        in_specs=[in_vmem] * 4,
        out_specs=(hbm,) * 4,
        scratch_shapes=[dma((4,))],
        compiler_params=pltpu.CompilerParams(vmem_limit_bytes=2**20),
    )(*results)
    return d_tokens, d_weight, d_gain.reshape(FEATS), d_log.reshape(ROWS)


def solution(mesh):
    in_specs = (
        P(("dp", "row"), "col"),
        P("col"),
        P("col", "row"),
        P(("dp", "col"), "row"),
        P(("dp", "row"), "col"),
    )
    out_specs = (P(("dp", "row"), "col"), P(("col", "dp"), "row"), P("col"), P(("dp", "row")))
    return jax.shard_map(local, mesh=mesh, in_specs=in_specs, out_specs=out_specs, check_vma=False)
```

```python
import jax
import jax.numpy as jnp
from jax import lax
from jax.experimental import pallas as pl
from jax.experimental.pallas import tpu as pltpu
from jax.sharding import PartitionSpec as P

MESH = pl.DeviceIdType.MESH
BF16, F32 = jnp.bfloat16, jnp.float32
D = 8192
TOKENS = 16384
ROWS = 512
FEATS = 2048
COLS = 1024
QUARTER = 256
SIDE = 4
SLABS = 8
CHUNKS = ((0, 1), (1, 1), (2, 2), (4, 2), (6, 2))
N = len(CHUNKS)
AHEAD = 3
LEAD = 2
STRAIGHT = ((0, 0), (0, 0), (0, 0), (0, 1), (1, 1))
ORDER = (
    ("M", 0), ("M", 1), ("P", 0), ("M", 2), ("P", 1), ("E", 0), ("normed", 0), ("M", 3), ("P", 2), ("E", 1), ("Q", 0), ("M", 4), ("normed", 1), ("P", 3), ("E", 2), ("Q", 1), ("F", 0), ("inner", 0), ("E", 3), ("E", 4), ("Q", 2), ("F", 1), ("gain", 0), ("F", 2), ("tokens", 0), ("F", 3), ("F", 4),
)
PARTS = (((0, 4), (0, 4)), ((4, 8), (4, 8)))
FIRST_PEER = 0


def dot(a, b, dims):
    return lax.dot_general(a, b, ((dims[:1], dims[1:]), ((), ())), preferred_element_type=F32)


def kernel(*refs):
    it = iter(refs)
    tok_hbm, gain_hbm, w_hbm, dout_hbm, dres_hbm = [next(it) for _ in range(5)]
    dtok_ref, dw_ref, dgain_ref, dlog_ref = [next(it) for _ in range(4)]
    tok, tok_peer, grads, other, w, w_peer, dn, dres, scaled_t = [next(it) for _ in range(9)]
    gain_flat, gain_row, lanes, sq, inv_row, inv_col, coef_col, inner_buf = [next(it) for _ in range(8)]
    dg_acc, dg_a, dg_b, dw_t = [next(it) for _ in range(4)]
    part, got1a, got1b, mid, got2a, got2b = [[next(it) for _ in range(N)] for _ in range(6)]
    local_sem, ag_s, ag_r, tp_s, tp_r, wp_s, wp_r, ot_s, ot_r = [next(it) for _ in range(9)]
    sq_s, sq_r, in_s, in_r, ga_s, ga_r, gb_s, gb_r, rs_s, rs_r = [next(it) for _ in range(10)]

    dp, r, z = lax.axis_index("dp"), lax.axis_index("row"), lax.axis_index("col")
    y, x = dp // SIDE, dp % SIDE

    def dev(dy=0, dx=0, dr=0, dz=0):
        return ((y + dy) % SIDE * SIDE + (x + dx) % SIDE, (r + dr) % 2, (z + dz) % SIDE)

    def send(src, dst, ss, rs, to):
        pltpu.make_async_remote_copy(
            src_ref=src, dst_ref=dst, send_sem=ss, recv_sem=rs, device_id=to, device_id_type=MESH
        ).start()

    def descriptor(ref, sem):
        return pltpu.make_async_remote_copy(
            src_ref=ref, dst_ref=ref, send_sem=sem, recv_sem=sem, device_id=dev(dr=1), device_id_type=MESH
        )

    def arrived(ref, sem):
        descriptor(ref, sem).wait_recv()

    def left(ref, sem):
        descriptor(ref, sem).wait_send()

    def load(src, dst, i):
        c = pltpu.make_async_copy(src, dst, local_sem.at[i])
        c.start()
        return c

    def slot(q):
        return pl.ds(pl.multiple_of((q + 2 * r) % SIDE * QUARTER, QUARTER), QUARTER)

    def half_slot(q, half):
        return pl.ds(pl.multiple_of((q + 2 * r) % SIDE * QUARTER + half * 128, 128), 128)

    def slabs(k):
        return pl.ds(*CHUNKS[k])

    partners = [dev(dr=1)]
    partners += [dev(dz=d) for d in (1, 2, 3)] + [dev(dr=1, dz=d) for d in (1, 2, 3)]
    partners += [dev(dx=d) for d in (1, 2, 3)] + [dev(dr=1, dx=d) for d in (1, 2, 3)]
    partners += [dev(dy=d) for d in (1, 2, 3)]
    barrier = pltpu.get_barrier_semaphore()
    for partner in partners:
        pl.semaphore_signal(barrier, inc=1, device_id=partner, device_id_type=MESH)

    for c in range(SLABS):
        load(dout_hbm.at[:, pl.ds(c * 128, 128)], grads.at[c, slot(z)], 1)
    tok_load = load(tok_hbm, tok, 0)
    gain_load = load(gain_hbm, gain_flat, 2)
    w_load = load(w_hbm, w, 3)
    res_load = load(dres_hbm, dres, 4)

    def gather_send(c):
        own = grads.at[c, slot(z)]
        for d in (1, 3) if c else (1, 3, 2):
            send(own, own, ag_s, ag_r.at[c, 0], dev(dz=d))

    relayed = [0]

    def gather_relay(hi):
        while relayed[0] < min(hi, SLABS - 1):
            relayed[0] += 1
            c = relayed[0]
            arrived(grads.at[c, pl.ds(0, 2 * QUARTER)], ag_r.at[c, 0])
            low, high = grads.at[c, half_slot(z + 1, 0)], grads.at[c, half_slot(z + 3, 1)]
            send(low, low, ag_s, ag_r.at[c, 1], dev(dz=3))
            send(high, high, ag_s, ag_r.at[c, 1], dev(dz=1))
            if c + AHEAD < SLABS:
                gather_send(c + AHEAD)

    def gather_wait(k):
        for c in range(CHUNKS[k][0], sum(CHUNKS[k])):
            if c == 0:
                arrived(grads.at[c, pl.ds(0, 3 * QUARTER)], ag_r.at[c, 0])
            else:
                gather_relay(c + LEAD)
                arrived(grads.at[c, pl.ds(0, QUARTER)], ag_r.at[c, 1])
        send(grads.at[slabs(k), pl.ds(ROWS, ROWS)], other.at[slabs(k)], ot_s, ot_r.at[k], dev(dr=1))

    own_quarter = grads.at[:, slot(z)]
    pltpu.make_async_copy(own_quarter, own_quarter, local_sem.at[1]).wait()
    pl.semaphore_wait(barrier, len(partners))
    gather_send(0)
    for b in range(SIDE):
        cols = pl.ds(b * 512, 512)
        send(tok_hbm.at[:, cols], tok_peer.at[:, cols], tp_s, tp_r.at[b], dev(dr=1))
    send(w_hbm, w_peer, wp_s, wp_r, dev(dr=1))

    tok_load.wait()

    @pl.loop(0, ROWS // 16)
    def _(i):
        rows = pl.ds(pl.multiple_of(i * 16, 16), 16)
        acc = jnp.zeros((16, 128), F32)
        for j in range(FEATS // 128):
            t = tok[rows, pl.ds(j * 128, 128)].astype(F32)
            acc += t * t
        lanes[rows, :] = acc

    def lane_sums():
        total = jnp.sum(lanes[...].T, axis=0, keepdims=True)
        return jnp.broadcast_to(total, (8, ROWS))

    own_sq = sq.at[z]
    own_sq[...] = lane_sums()
    peer_sq = sq.at[SIDE + z]
    for d in (1, 2, 3):
        send(own_sq, own_sq, sq_s, sq_r, dev(dz=d))
        send(own_sq, peer_sq, sq_s, sq_r, dev(dr=1, dz=d))
    send(own_sq, peer_sq, sq_s, sq_r, dev(dr=1))
    for c in range(1, AHEAD + 1):
        gather_send(c)

    gain_load.wait()
    gain_row[...] = gain_flat[...].astype(F32).reshape(1, FEATS)

    arrived(sq.at[pl.ds(0, 7)], sq_r)
    for side in range(2):
        total = sq[4 * side] + sq[4 * side + 1] + sq[4 * side + 2] + sq[4 * side + 3]
        inv_row[:, pl.ds(side * ROWS, ROWS)] = lax.rsqrt(total * (1.0 / D) + 1e-05)

    def as_column(row):
        return jnp.broadcast_to(row[0:1], (128, ROWS)).T

    def product(k):
        first, count = CHUNKS[k]
        width, cq = count * 128, count * 32
        for c in range(count):
            for s in range(SIDE):
                toks = pl.ds(s * QUARTER, QUARTER)
                g = grads[first + c, toks, :].T.astype(F32)
                scaled_t[pl.ds(c * 128, 128), toks] = (g * inv_row[0:1, toks]).astype(BF16)

        def block(b):
            feats = pl.ds(b * 512, 512) if isinstance(b, int) else pl.ds(pl.multiple_of(b * 512, 512), 512)
            res = dot(scaled_t[pl.ds(0, width), pl.ds(0, ROWS)], tok[:, feats], (1, 0))
            res += dot(scaled_t[pl.ds(0, width), pl.ds(ROWS, ROWS)], tok_peer[:, feats], (1, 0))
            res = res.astype(BF16)
            for j in range(SIDE):
                for h in range(2):
                    for u in range(2):
                        lo = (2 * h + u) * cq
                        piece = res[lo : lo + cq, j * 128 : j * 128 + 128]
                        if h == 0:
                            part[k][h, j, u, b] = piece
                        else:
                            part[k][h, b, u, j] = piece

        if k == 0:
            for b in range(SIDE):
                arrived(tok_peer.at[:, pl.ds(b * 512, 512)], tp_r.at[b])
                block(b)
                if b > 0:
                    gather_relay(b)
        else:
            pl.loop(0, SIDE)(block)

    def axis(h, stage):
        if (h == 0) == (stage == 0):
            return x, (lambda d: dev(dx=d))
        return y, (lambda d: dev(dy=d))

    def buffers(stage):
        return (part, got1a, got1b) if stage == 0 else (mid, got2a, got2b)

    def reduce_start(k, stage):
        src, got_a, got_b = buffers(stage)
        ss, rs = rs_s.at[k, stage], rs_r.at[k, stage]
        for h in range(2):
            m, to = axis(h, stage)
            far, up, down = (m + 2) % SIDE, (m + 1) % SIDE, (m + 3) % SIDE
            if STRAIGHT[k][stage]:
                send(src[k].at[h, far], got_b[k].at[h, 1], ss, rs.at[0], to(2))
                send(src[k].at[h, up], got_b[k].at[h, 0], ss, rs.at[0], to(1))
                send(src[k].at[h, down], got_b[k].at[h, 2], ss, rs.at[0], to(3))
                continue
            send(src[k].at[h, far, 0], got_a[k].at[h, 0], ss, rs.at[1], to(1))
            send(src[k].at[h, far, 1], got_a[k].at[h, 1], ss, rs.at[1], to(3))
            send(src[k].at[h, up, 1], got_b[k].at[h, 0, 1], ss, rs.at[0], to(1))
            send(src[k].at[h, down, 0], got_b[k].at[h, 1, 0], ss, rs.at[0], to(3))

    def add(a, b):
        return (a.astype(F32) + b.astype(F32)).astype(BF16)

    def reduce_pass(k, stage):
        if STRAIGHT[k][stage]:
            return
        src, got_a, got_b = buffers(stage)
        ss, rs = rs_s.at[k, stage], rs_r.at[k, stage]
        arrived(got_a[k], rs.at[1])
        for h in range(2):
            m, to = axis(h, stage)
            up, down = (m + 1) % SIDE, (m + 3) % SIDE
            src[k][h, up, 0] = add(src[k][h, up, 0], got_a[k][h, 0])
            send(src[k].at[h, up, 0], got_b[k].at[h, 0, 0], ss, rs.at[0], to(1))
            src[k][h, down, 1] = add(src[k][h, down, 1], got_a[k][h, 1])
            send(src[k].at[h, down, 1], got_b[k].at[h, 1, 1], ss, rs.at[0], to(3))

    def reduce_end(k, stage):
        src, _, got_b = buffers(stage)
        cq = CHUNKS[k][1] * 32
        arrived(got_b[k], rs_r.at[k, stage, 0])
        for h in range(2):
            m, _ = axis(h, stage)
            for u in range(2):
                total = src[k][h, m, u].astype(F32)
                for d in range(3 if STRAIGHT[k][stage] else 2):
                    total += got_b[k][h, d, u].astype(F32)
                if stage == 0:
                    for t in range(SIDE):
                        mid[k][h, t, u] = total[t].astype(BF16)
                else:
                    dw_t[pl.ds((2 * h + u) * cq, cq), :] = total

    def finish(k):
        first, count = CHUNKS[k]
        own = gain_row[0:1, pl.ds(pl.multiple_of(dp * 128, 128), 128)] * float(TOKENS) ** (-0.5)
        dw_ref[:, pl.ds(first * 128, count * 128)] = (dw_t[pl.ds(0, count * 128), :] * own).T.astype(BF16)

    def normed_grad(p):
        sources = [(grads, w, PARTS[p][0]), (other, w_peer, PARTS[p][1])]
        if PARTS[p][1]:
            for k in range(N):
                if CHUNKS[k][0] in range(*PARTS[p][1]):
                    arrived(other.at[slabs(k)], ot_r.at[k])
        if p == 0:
            w_load.wait()
        if p == FIRST_PEER:
            arrived(w_peer, wp_r)

        @pl.loop(0, SIDE)
        def _(b):
            feats = pl.ds(pl.multiple_of(b * 512, 512), 512)
            res = None
            for rows, weights, span in sources:
                if span:
                    left_side = jnp.concatenate([rows[c, pl.ds(0, ROWS), :] for c in range(*span)], axis=1)
                    right_side = weights[feats, pl.ds(span[0] * 128, (span[1] - span[0]) * 128)]
                    term = dot(left_side, right_side, (1, 1))
                    res = term if res is None else res + term
            if p == 0:
                dn[:, feats] = res
            else:
                dn[:, feats] += res

    def inner_start():
        inv_col[...] = as_column(inv_row[:, 0:ROWS])
        dg_acc[...] = jnp.zeros_like(dg_acc)

        @pl.loop(0, ROWS // 16)
        def _(i):
            rows = pl.ds(pl.multiple_of(i * 16, 16), 16)
            inv = inv_col[rows, :]
            acc = jnp.zeros((16, 128), F32)
            for j in range(FEATS // 128):
                cols = pl.ds(j * 128, 128)
                prod = dn[rows, cols] * tok[rows, cols].astype(F32)
                acc += prod * gain_row[0:1, cols]
                prod = prod * inv
                dg_acc[:, cols] += prod[0:8] + prod[8:16]
            lanes[rows, :] = acc

        own_inner = inner_buf.at[z]
        own_inner[...] = lane_sums()
        for d in (1, 2, 3):
            send(own_inner, own_inner, in_s, in_r, dev(dz=d))
        own_dg = dg_a.at[r * SIDE + x]
        for j in range(FEATS // 128):
            own_dg[pl.ds(j, 1), :] = jnp.sum(dg_acc[:, pl.ds(j * 128, 128)], axis=0, keepdims=True)
        for d in (1, 2, 3):
            send(own_dg, own_dg, ga_s, ga_r, dev(dx=d))
            send(own_dg, own_dg, ga_s, ga_r, dev(dr=1, dx=d))
        send(own_dg, own_dg, ga_s, ga_r, dev(dr=1))

    def gain_y():
        arrived(dg_a.at[pl.ds(0, 7)], ga_r)
        total = dg_a[0]
        for i in range(1, 8):
            total += dg_a[i]
        own_dg = dg_b.at[y]
        own_dg[...] = total
        for d in (1, 2, 3):
            send(own_dg, own_dg, gb_s, gb_r, dev(dy=d))

    def gain_end():
        arrived(dg_b.at[pl.ds(0, 3)], gb_r)
        dgain_ref[...] = (dg_b[0] + dg_b[1] + dg_b[2] + dg_b[3]) * float(TOKENS) ** (-0.5)

    def tokens_end():
        arrived(inner_buf.at[pl.ds(0, 3)], in_r)
        inner = inner_buf[0] + inner_buf[1] + inner_buf[2] + inner_buf[3]
        inv = inv_row[:, 0:ROWS]
        log_scale = inner * inv * float(D) ** (-0.5)
        for j in range(SIDE):
            dlog_ref[pl.ds(j, 1), :] = log_scale[0:1, j * 128 : j * 128 + 128]
        coef_col[...] = as_column(inv * inv * inv * inner * (1.0 / D))
        res_load.wait()

        @pl.loop(0, ROWS // 16)
        def _(i):
            rows = pl.ds(pl.multiple_of(i * 16, 16), 16)
            inv_c, coef = inv_col[rows, :], coef_col[rows, :]
            for j in range(FEATS // 128):
                cols = pl.ds(j * 128, 128)
                scaled = dn[rows, cols] * gain_row[0:1, cols]
                value = dres[rows, cols].astype(F32) + inv_c * scaled
                dtok_ref[rows, cols] = (value - tok[rows, cols].astype(F32) * coef).astype(BF16)

    def step(k, n):
        if n == 0:
            gather_wait(k)
            product(k)
            reduce_start(k, 0)
            gather_relay(sum(CHUNKS[k]) + LEAD)
        if n == 1:
            reduce_pass(k, 0)
        if n == 2:
            reduce_end(k, 0)
            reduce_start(k, 1)
        if n == 3:
            reduce_pass(k, 1)
        if n == 4:
            reduce_end(k, 1)
            finish(k)

    for what, k in ORDER:
        if what == "normed":
            normed_grad(k)
        elif what == "inner":
            inner_start()
        elif what == "tokens":
            tokens_end()
        elif what == "gain":
            gain_y()
        else:
            step(k, "MPEQF".index(what))
    gain_end()
    left(grads.at[pl.ds(0, 6)], ag_s)
    left(tok_peer, tp_s)
    left(w_peer, wp_s)
    left(other, ot_s)
    left(sq.at[pl.ds(0, 7)], sq_s)
    left(inner_buf.at[pl.ds(0, 3)], in_s)
    left(dg_a.at[pl.ds(0, 7)], ga_s)
    left(dg_b.at[pl.ds(0, 3)], gb_s)
    for k in range(N):
        left(part[k].at[:, pl.ds(0, 3)], rs_s.at[k, 0])
        left(mid[k].at[:, pl.ds(0, 3)], rs_s.at[k, 1])


def write_out(dtok, dw, dgain, dlog, dtok_hbm, dw_hbm, dgain_hbm, dlog_hbm, sem):
    pairs = ((dtok, dtok_hbm), (dw, dw_hbm), (dgain, dgain_hbm), (dlog, dlog_hbm))
    copies = [pltpu.make_async_copy(src, dst, sem.at[i]) for i, (src, dst) in enumerate(pairs)]
    for c in copies:
        c.start()
    for c in copies:
        c.wait()


def local(tokens, gain, weight, d_out, d_residual):
    vmem, dma = pltpu.VMEM, pltpu.SemaphoreType.DMA
    cqs = [count * 32 for _, count in CHUNKS]
    scratch = [
        vmem((ROWS, FEATS), BF16),
        vmem((ROWS, FEATS), BF16),
        vmem((SLABS, 2 * ROWS, 128), BF16),
        vmem((SLABS, ROWS, 128), BF16),
        vmem((FEATS, COLS), BF16),
        vmem((FEATS, COLS), BF16),
        vmem((ROWS, FEATS), F32),
        vmem((ROWS, FEATS), BF16),
        vmem((256, 2 * ROWS), BF16),
        vmem((FEATS,), BF16),
        vmem((1, FEATS), F32),
        vmem((ROWS, 128), F32),
        vmem((2 * SIDE, 8, ROWS), F32),
        vmem((8, 2 * ROWS), F32),
        vmem((ROWS, 128), F32),
        vmem((ROWS, 128), F32),
        vmem((SIDE, 8, ROWS), F32),
        vmem((8, FEATS), F32),
        vmem((2 * SIDE, 16, 128), F32),
        vmem((SIDE, 16, 128), F32),
        vmem((256, 128), F32),
    ]
    scratch += [vmem((2, SIDE, 2, SIDE, c, 128), BF16) for c in cqs]
    scratch += [vmem((2, 2, SIDE, c, 128), BF16) for c in cqs]
    scratch += [vmem((2, 2 + s[0], 2, SIDE, c, 128), BF16) for c, s in zip(cqs, STRAIGHT)]
    scratch += [vmem((2, SIDE, 2, c, 128), BF16) for c in cqs]
    scratch += [vmem((2, 2, c, 128), BF16) for c in cqs]
    scratch += [vmem((2, 2 + s[1], 2, c, 128), BF16) for c, s in zip(cqs, STRAIGHT)]
    scratch += [
        dma((5,)),
        dma,
        dma((SLABS, 2)),
        dma,
        dma((SIDE,)),
        dma,
        dma,
        dma,
        dma((N,)),
        dma,
        dma,
        dma,
        dma,
        dma,
        dma,
        dma,
        dma,
        dma((N, 2)),
        dma((N, 2, 2)),
    ]
    hbm, in_vmem = pl.BlockSpec(memory_space=pltpu.HBM), pl.BlockSpec(memory_space=pltpu.VMEM)
    shapes = (((ROWS, FEATS), BF16), ((128, COLS), BF16), ((16, 128), F32), ((4, 128), F32))
    results = pl.pallas_call(
        kernel,
        name="fused",
        out_shape=tuple(pltpu.VMEM(*shape) for shape in shapes),
        in_specs=[hbm] * 5,
        out_specs=(in_vmem,) * 4,
        scratch_shapes=scratch,
        compiler_params=pltpu.CompilerParams(
            collective_id=0, has_side_effects=True, vmem_limit_bytes=48 * 2**20
        ),
        cost_estimate=pl.CostEstimate(flops=8 * 2**30, bytes_accessed=12 * 2**20, transcendentals=0),
    )(*[pltpu.with_memory_space_constraint(a, pltpu.HBM) for a in (tokens, gain, weight, d_out, d_residual)])
    d_tokens, d_weight, d_gain, d_log = pl.pallas_call(
        write_out,
        name="write_out",
        out_shape=tuple(jax.ShapeDtypeStruct(*shape) for shape in shapes),
        in_specs=[in_vmem] * 4,
        out_specs=(hbm,) * 4,
        scratch_shapes=[dma((4,))],
        compiler_params=pltpu.CompilerParams(vmem_limit_bytes=2**20),
    )(*results)
    return d_tokens, d_weight, d_gain.reshape(FEATS), d_log.reshape(ROWS)


def solution(mesh):
    in_specs = (
        P(("dp", "row"), "col"),
        P("col"),
        P("col", "row"),
        P(("dp", "col"), "row"),
        P(("dp", "row"), "col"),
    )
    out_specs = (P(("dp", "row"), "col"), P(("col", "dp"), "row"), P("col"), P(("dp", "row")))
    return jax.shard_map(local, mesh=mesh, in_specs=in_specs, out_specs=out_specs, check_vma=False)
```

```python
import jax
import jax.numpy as jnp
from jax import lax
from jax.experimental import pallas as pl
from jax.experimental.pallas import tpu as pltpu
from jax.sharding import PartitionSpec as P

MESH = pl.DeviceIdType.MESH
BF16, F32 = jnp.bfloat16, jnp.float32
D = 8192
TOKENS = 16384
ROWS = 512
FEATS = 2048
COLS = 1024
QUARTER = 256
SIDE = 4
SLABS = 8
CHUNKS = ((0, 1), (1, 1), (2, 2), (4, 2), (6, 2))
N = len(CHUNKS)
AHEAD = 3
LEAD = 2
STRAIGHT = ((0, 0), (0, 0), (0, 0), (0, 1), (1, 1))
ORDER = (
    ("M", 0), ("M", 1), ("P", 0), ("M", 2), ("P", 1), ("E", 0), ("normed", 0), ("M", 3), ("P", 2), ("E", 1), ("Q", 0), ("M", 4), ("normed", 1), ("inner", 0), ("P", 3), ("E", 2), ("Q", 1), ("F", 0), ("E", 3), ("E", 4), ("Q", 2), ("F", 1), ("gain", 0), ("tokens", 0), ("F", 2), ("F", 3), ("F", 4),
)
PARTS = (((0, 4), (0, 4)), ((4, 8), (4, 8)))
FIRST_PEER = 0


def dot(a, b, dims):
    return lax.dot_general(a, b, ((dims[:1], dims[1:]), ((), ())), preferred_element_type=F32)


def kernel(*refs):
    it = iter(refs)
    tok_hbm, gain_hbm, w_hbm, dout_hbm, dres_hbm = [next(it) for _ in range(5)]
    dtok_ref, dw_ref, dgain_ref, dlog_ref = [next(it) for _ in range(4)]
    tok, tok_peer, grads, other, w, w_peer, dn, dres, scaled_t = [next(it) for _ in range(9)]
    gain_flat, gain_row, lanes, sq, inv_row, inv_col, coef_col, inner_buf = [next(it) for _ in range(8)]
    dg_acc, dg_a, dg_b, dw_t = [next(it) for _ in range(4)]
    part, got1a, got1b, mid, got2a, got2b = [[next(it) for _ in range(N)] for _ in range(6)]
    local_sem, ag_s, ag_r, tp_s, tp_r, wp_s, wp_r, ot_s, ot_r = [next(it) for _ in range(9)]
    sq_s, sq_r, in_s, in_r, ga_s, ga_r, gb_s, gb_r, rs_s, rs_r = [next(it) for _ in range(10)]

    dp, r, z = lax.axis_index("dp"), lax.axis_index("row"), lax.axis_index("col")
    y, x = dp // SIDE, dp % SIDE

    def dev(dy=0, dx=0, dr=0, dz=0):
        return ((y + dy) % SIDE * SIDE + (x + dx) % SIDE, (r + dr) % 2, (z + dz) % SIDE)

    def send(src, dst, ss, rs, to):
        pltpu.make_async_remote_copy(
            src_ref=src, dst_ref=dst, send_sem=ss, recv_sem=rs, device_id=to, device_id_type=MESH
        ).start()

    def descriptor(ref, sem):
        return pltpu.make_async_remote_copy(
            src_ref=ref, dst_ref=ref, send_sem=sem, recv_sem=sem, device_id=dev(dr=1), device_id_type=MESH
        )

    def arrived(ref, sem):
        descriptor(ref, sem).wait_recv()

    def left(ref, sem):
        descriptor(ref, sem).wait_send()

    def load(src, dst, i):
        c = pltpu.make_async_copy(src, dst, local_sem.at[i])
        c.start()
        return c

    def slot(q):
        return pl.ds(pl.multiple_of((q + 2 * r) % SIDE * QUARTER, QUARTER), QUARTER)

    def half_slot(q, half):
        return pl.ds(pl.multiple_of((q + 2 * r) % SIDE * QUARTER + half * 128, 128), 128)

    def slabs(k):
        return pl.ds(*CHUNKS[k])

    partners = [dev(dr=1)]
    partners += [dev(dz=d) for d in (1, 2, 3)] + [dev(dr=1, dz=d) for d in (1, 2, 3)]
    partners += [dev(dx=d) for d in (1, 2, 3)] + [dev(dr=1, dx=d) for d in (1, 2, 3)]
    partners += [dev(dy=d) for d in (1, 2, 3)]
    barrier = pltpu.get_barrier_semaphore()
    for partner in partners:
        pl.semaphore_signal(barrier, inc=1, device_id=partner, device_id_type=MESH)

    for c in range(SLABS):
        load(dout_hbm.at[:, pl.ds(c * 128, 128)], grads.at[c, slot(z)], 1)
    tok_load = load(tok_hbm, tok, 0)
    gain_load = load(gain_hbm, gain_flat, 2)
    w_load = load(w_hbm, w, 3)
    res_load = load(dres_hbm, dres, 4)

    def gather_send(c):
        own = grads.at[c, slot(z)]
        for d in (1, 3) if c else (1, 3, 2):
            send(own, own, ag_s, ag_r.at[c, 0], dev(dz=d))

    relayed = [0]

    def gather_relay(hi):
        while relayed[0] < min(hi, SLABS - 1):
            relayed[0] += 1
            c = relayed[0]
            arrived(grads.at[c, pl.ds(0, 2 * QUARTER)], ag_r.at[c, 0])
            low, high = grads.at[c, half_slot(z + 1, 0)], grads.at[c, half_slot(z + 3, 1)]
            send(low, low, ag_s, ag_r.at[c, 1], dev(dz=3))
            send(high, high, ag_s, ag_r.at[c, 1], dev(dz=1))
            if c + AHEAD < SLABS:
                gather_send(c + AHEAD)

    def gather_wait(k):
        for c in range(CHUNKS[k][0], sum(CHUNKS[k])):
            if c == 0:
                arrived(grads.at[c, pl.ds(0, 3 * QUARTER)], ag_r.at[c, 0])
            else:
                gather_relay(c + LEAD)
                arrived(grads.at[c, pl.ds(0, QUARTER)], ag_r.at[c, 1])
        send(grads.at[slabs(k), pl.ds(ROWS, ROWS)], other.at[slabs(k)], ot_s, ot_r.at[k], dev(dr=1))

    own_quarter = grads.at[:, slot(z)]
    pltpu.make_async_copy(own_quarter, own_quarter, local_sem.at[1]).wait()
    pl.semaphore_wait(barrier, len(partners))
    gather_send(0)
    for b in range(SIDE):
        cols = pl.ds(b * 512, 512)
        send(tok_hbm.at[:, cols], tok_peer.at[:, cols], tp_s, tp_r.at[b], dev(dr=1))
    send(w_hbm, w_peer, wp_s, wp_r, dev(dr=1))

    tok_load.wait()

    @pl.loop(0, ROWS // 16)
    def _(i):
        rows = pl.ds(pl.multiple_of(i * 16, 16), 16)
        acc = jnp.zeros((16, 128), F32)
        for j in range(FEATS // 128):
            t = tok[rows, pl.ds(j * 128, 128)].astype(F32)
            acc += t * t
        lanes[rows, :] = acc

    def lane_sums():
        total = jnp.sum(lanes[...].T, axis=0, keepdims=True)
        return jnp.broadcast_to(total, (8, ROWS))

    own_sq = sq.at[z]
    own_sq[...] = lane_sums()
    peer_sq = sq.at[SIDE + z]
    for d in (1, 2, 3):
        send(own_sq, own_sq, sq_s, sq_r, dev(dz=d))
        send(own_sq, peer_sq, sq_s, sq_r, dev(dr=1, dz=d))
    send(own_sq, peer_sq, sq_s, sq_r, dev(dr=1))
    for c in range(1, AHEAD + 1):
        gather_send(c)

    gain_load.wait()
    gain_row[...] = gain_flat[...].astype(F32).reshape(1, FEATS)

    arrived(sq.at[pl.ds(0, 7)], sq_r)
    for side in range(2):
        total = sq[4 * side] + sq[4 * side + 1] + sq[4 * side + 2] + sq[4 * side + 3]
        inv_row[:, pl.ds(side * ROWS, ROWS)] = lax.rsqrt(total * (1.0 / D) + 1e-05)

    def as_column(row):
        return jnp.broadcast_to(row[0:1], (128, ROWS)).T

    def product(k):
        first, count = CHUNKS[k]
        width, cq = count * 128, count * 32
        for c in range(count):
            for s in range(SIDE):
                toks = pl.ds(s * QUARTER, QUARTER)
                g = grads[first + c, toks, :].T.astype(F32)
                scaled_t[pl.ds(c * 128, 128), toks] = (g * inv_row[0:1, toks]).astype(BF16)

        def block(b):
            feats = pl.ds(b * 512, 512) if isinstance(b, int) else pl.ds(pl.multiple_of(b * 512, 512), 512)
            res = dot(scaled_t[pl.ds(0, width), pl.ds(0, ROWS)], tok[:, feats], (1, 0))
            res += dot(scaled_t[pl.ds(0, width), pl.ds(ROWS, ROWS)], tok_peer[:, feats], (1, 0))
            res = res.astype(BF16)
            for j in range(SIDE):
                for h in range(2):
                    for u in range(2):
                        lo = (2 * h + u) * cq
                        piece = res[lo : lo + cq, j * 128 : j * 128 + 128]
                        if h == 0:
                            part[k][h, j, u, b] = piece
                        else:
                            part[k][h, b, u, j] = piece

        if k == 0:
            for b in range(SIDE):
                arrived(tok_peer.at[:, pl.ds(b * 512, 512)], tp_r.at[b])
                block(b)
                if b > 0:
                    gather_relay(b)
        else:
            pl.loop(0, SIDE)(block)

    def axis(h, stage):
        if (h == 0) == (stage == 0):
            return x, (lambda d: dev(dx=d))
        return y, (lambda d: dev(dy=d))

    def buffers(stage):
        return (part, got1a, got1b) if stage == 0 else (mid, got2a, got2b)

    def reduce_start(k, stage):
        src, got_a, got_b = buffers(stage)
        ss, rs = rs_s.at[k, stage], rs_r.at[k, stage]
        for h in range(2):
            m, to = axis(h, stage)
            far, up, down = (m + 2) % SIDE, (m + 1) % SIDE, (m + 3) % SIDE
            if STRAIGHT[k][stage]:
                send(src[k].at[h, far], got_b[k].at[h, 1], ss, rs.at[0], to(2))
                send(src[k].at[h, up], got_b[k].at[h, 0], ss, rs.at[0], to(1))
                send(src[k].at[h, down], got_b[k].at[h, 2], ss, rs.at[0], to(3))
                continue
            send(src[k].at[h, far, 0], got_a[k].at[h, 0], ss, rs.at[1], to(1))
            send(src[k].at[h, far, 1], got_a[k].at[h, 1], ss, rs.at[1], to(3))
            send(src[k].at[h, up, 1], got_b[k].at[h, 0, 1], ss, rs.at[0], to(1))
            send(src[k].at[h, down, 0], got_b[k].at[h, 1, 0], ss, rs.at[0], to(3))

    def add(a, b):
        return (a.astype(F32) + b.astype(F32)).astype(BF16)

    def reduce_pass(k, stage):
        if STRAIGHT[k][stage]:
            return
        src, got_a, got_b = buffers(stage)
        ss, rs = rs_s.at[k, stage], rs_r.at[k, stage]
        arrived(got_a[k], rs.at[1])
        for h in range(2):
            m, to = axis(h, stage)
            up, down = (m + 1) % SIDE, (m + 3) % SIDE
            src[k][h, up, 0] = add(src[k][h, up, 0], got_a[k][h, 0])
            send(src[k].at[h, up, 0], got_b[k].at[h, 0, 0], ss, rs.at[0], to(1))
            src[k][h, down, 1] = add(src[k][h, down, 1], got_a[k][h, 1])
            send(src[k].at[h, down, 1], got_b[k].at[h, 1, 1], ss, rs.at[0], to(3))

    def reduce_end(k, stage):
        src, _, got_b = buffers(stage)
        cq = CHUNKS[k][1] * 32
        arrived(got_b[k], rs_r.at[k, stage, 0])
        for h in range(2):
            m, _ = axis(h, stage)
            for u in range(2):
                total = src[k][h, m, u].astype(F32)
                for d in range(3 if STRAIGHT[k][stage] else 2):
                    total += got_b[k][h, d, u].astype(F32)
                if stage == 0:
                    for t in range(SIDE):
                        mid[k][h, t, u] = total[t].astype(BF16)
                else:
                    dw_t[pl.ds((2 * h + u) * cq, cq), :] = total

    def finish(k):
        first, count = CHUNKS[k]
        own = gain_row[0:1, pl.ds(pl.multiple_of(dp * 128, 128), 128)] * float(TOKENS) ** (-0.5)
        dw_ref[:, pl.ds(first * 128, count * 128)] = (dw_t[pl.ds(0, count * 128), :] * own).T.astype(BF16)

    def normed_grad(p):
        sources = [(grads, w, PARTS[p][0]), (other, w_peer, PARTS[p][1])]
        if PARTS[p][1]:
            for k in range(N):
                if CHUNKS[k][0] in range(*PARTS[p][1]):
                    arrived(other.at[slabs(k)], ot_r.at[k])
        if p == 0:
            w_load.wait()
        if p == FIRST_PEER:
            arrived(w_peer, wp_r)

        @pl.loop(0, SIDE)
        def _(b):
            feats = pl.ds(pl.multiple_of(b * 512, 512), 512)
            res = None
            for rows, weights, span in sources:
                if span:
                    left_side = jnp.concatenate([rows[c, pl.ds(0, ROWS), :] for c in range(*span)], axis=1)
                    right_side = weights[feats, pl.ds(span[0] * 128, (span[1] - span[0]) * 128)]
                    term = dot(left_side, right_side, (1, 1))
                    res = term if res is None else res + term
            if p == 0:
                dn[:, feats] = res
            else:
                dn[:, feats] += res

    def inner_start():
        inv_col[...] = as_column(inv_row[:, 0:ROWS])
        dg_acc[...] = jnp.zeros_like(dg_acc)

        @pl.loop(0, ROWS // 16)
        def _(i):
            rows = pl.ds(pl.multiple_of(i * 16, 16), 16)
            inv = inv_col[rows, :]
            acc = jnp.zeros((16, 128), F32)
            for j in range(FEATS // 128):
                cols = pl.ds(j * 128, 128)
                prod = dn[rows, cols] * tok[rows, cols].astype(F32)
                acc += prod * gain_row[0:1, cols]
                prod = prod * inv
                dg_acc[:, cols] += prod[0:8] + prod[8:16]
            lanes[rows, :] = acc

        own_inner = inner_buf.at[z]
        own_inner[...] = lane_sums()
        for d in (1, 2, 3):
            send(own_inner, own_inner, in_s, in_r, dev(dz=d))
        own_dg = dg_a.at[r * SIDE + x]
        for j in range(FEATS // 128):
            own_dg[pl.ds(j, 1), :] = jnp.sum(dg_acc[:, pl.ds(j * 128, 128)], axis=0, keepdims=True)
        for d in (1, 2, 3):
            send(own_dg, own_dg, ga_s, ga_r, dev(dx=d))
            send(own_dg, own_dg, ga_s, ga_r, dev(dr=1, dx=d))
        send(own_dg, own_dg, ga_s, ga_r, dev(dr=1))

    def gain_y():
        arrived(dg_a.at[pl.ds(0, 7)], ga_r)
        total = dg_a[0]
        for i in range(1, 8):
            total += dg_a[i]
        own_dg = dg_b.at[y]
        own_dg[...] = total
        for d in (1, 2, 3):
            send(own_dg, own_dg, gb_s, gb_r, dev(dy=d))

    def gain_end():
        arrived(dg_b.at[pl.ds(0, 3)], gb_r)
        dgain_ref[...] = (dg_b[0] + dg_b[1] + dg_b[2] + dg_b[3]) * float(TOKENS) ** (-0.5)

    def tokens_end():
        arrived(inner_buf.at[pl.ds(0, 3)], in_r)
        inner = inner_buf[0] + inner_buf[1] + inner_buf[2] + inner_buf[3]
        inv = inv_row[:, 0:ROWS]
        log_scale = inner * inv * float(D) ** (-0.5)
        for j in range(SIDE):
            dlog_ref[pl.ds(j, 1), :] = log_scale[0:1, j * 128 : j * 128 + 128]
        coef_col[...] = as_column(inv * inv * inv * inner * (1.0 / D))
        res_load.wait()

        @pl.loop(0, ROWS // 16)
        def _(i):
            rows = pl.ds(pl.multiple_of(i * 16, 16), 16)
            inv_c, coef = inv_col[rows, :], coef_col[rows, :]
            for j in range(FEATS // 128):
                cols = pl.ds(j * 128, 128)
                scaled = dn[rows, cols] * gain_row[0:1, cols]
                value = dres[rows, cols].astype(F32) + inv_c * scaled
                dtok_ref[rows, cols] = (value - tok[rows, cols].astype(F32) * coef).astype(BF16)

    def step(k, n):
        if n == 0:
            gather_wait(k)
            product(k)
            reduce_start(k, 0)
            gather_relay(sum(CHUNKS[k]) + LEAD)
        if n == 1:
            reduce_pass(k, 0)
        if n == 2:
            reduce_end(k, 0)
            reduce_start(k, 1)
        if n == 3:
            reduce_pass(k, 1)
        if n == 4:
            reduce_end(k, 1)
            finish(k)

    for what, k in ORDER:
        if what == "normed":
            normed_grad(k)
        elif what == "inner":
            inner_start()
        elif what == "tokens":
            tokens_end()
        elif what == "gain":
            gain_y()
        else:
            step(k, "MPEQF".index(what))
    gain_end()
    left(grads.at[pl.ds(0, 6)], ag_s)
    left(tok_peer, tp_s)
    left(w_peer, wp_s)
    left(other, ot_s)
    left(sq.at[pl.ds(0, 7)], sq_s)
    left(inner_buf.at[pl.ds(0, 3)], in_s)
    left(dg_a.at[pl.ds(0, 7)], ga_s)
    left(dg_b.at[pl.ds(0, 3)], gb_s)
    for k in range(N):
        left(part[k].at[:, pl.ds(0, 3)], rs_s.at[k, 0])
        left(mid[k].at[:, pl.ds(0, 3)], rs_s.at[k, 1])


def write_out(dtok, dw, dgain, dlog, dtok_hbm, dw_hbm, dgain_hbm, dlog_hbm, sem):
    pairs = ((dtok, dtok_hbm), (dw, dw_hbm), (dgain, dgain_hbm), (dlog, dlog_hbm))
    copies = [pltpu.make_async_copy(src, dst, sem.at[i]) for i, (src, dst) in enumerate(pairs)]
    for c in copies:
        c.start()
    for c in copies:
        c.wait()


def local(tokens, gain, weight, d_out, d_residual):
    vmem, dma = pltpu.VMEM, pltpu.SemaphoreType.DMA
    cqs = [count * 32 for _, count in CHUNKS]
    scratch = [
        vmem((ROWS, FEATS), BF16),
        vmem((ROWS, FEATS), BF16),
        vmem((SLABS, 2 * ROWS, 128), BF16),
        vmem((SLABS, ROWS, 128), BF16),
        vmem((FEATS, COLS), BF16),
        vmem((FEATS, COLS), BF16),
        vmem((ROWS, FEATS), F32),
        vmem((ROWS, FEATS), BF16),
        vmem((256, 2 * ROWS), BF16),
        vmem((FEATS,), BF16),
        vmem((1, FEATS), F32),
        vmem((ROWS, 128), F32),
        vmem((2 * SIDE, 8, ROWS), F32),
        vmem((8, 2 * ROWS), F32),
        vmem((ROWS, 128), F32),
        vmem((ROWS, 128), F32),
        vmem((SIDE, 8, ROWS), F32),
        vmem((8, FEATS), F32),
        vmem((2 * SIDE, 16, 128), F32),
        vmem((SIDE, 16, 128), F32),
        vmem((256, 128), F32),
    ]
    scratch += [vmem((2, SIDE, 2, SIDE, c, 128), BF16) for c in cqs]
    scratch += [vmem((2, 2, SIDE, c, 128), BF16) for c in cqs]
    scratch += [vmem((2, 2 + s[0], 2, SIDE, c, 128), BF16) for c, s in zip(cqs, STRAIGHT)]
    scratch += [vmem((2, SIDE, 2, c, 128), BF16) for c in cqs]
    scratch += [vmem((2, 2, c, 128), BF16) for c in cqs]
    scratch += [vmem((2, 2 + s[1], 2, c, 128), BF16) for c, s in zip(cqs, STRAIGHT)]
    scratch += [
        dma((5,)),
        dma,
        dma((SLABS, 2)),
        dma,
        dma((SIDE,)),
        dma,
        dma,
        dma,
        dma((N,)),
        dma,
        dma,
        dma,
        dma,
        dma,
        dma,
        dma,
        dma,
        dma((N, 2)),
        dma((N, 2, 2)),
    ]
    hbm, in_vmem = pl.BlockSpec(memory_space=pltpu.HBM), pl.BlockSpec(memory_space=pltpu.VMEM)
    shapes = (((ROWS, FEATS), BF16), ((128, COLS), BF16), ((16, 128), F32), ((4, 128), F32))
    results = pl.pallas_call(
        kernel,
        name="fused",
        out_shape=tuple(pltpu.VMEM(*shape) for shape in shapes),
        in_specs=[hbm] * 5,
        out_specs=(in_vmem,) * 4,
        scratch_shapes=scratch,
        compiler_params=pltpu.CompilerParams(
            collective_id=0, has_side_effects=True, vmem_limit_bytes=48 * 2**20
        ),
        cost_estimate=pl.CostEstimate(flops=8 * 2**30, bytes_accessed=12 * 2**20, transcendentals=0),
    )(*[pltpu.with_memory_space_constraint(a, pltpu.HBM) for a in (tokens, gain, weight, d_out, d_residual)])
    d_tokens, d_weight, d_gain, d_log = pl.pallas_call(
        write_out,
        name="write_out",
        out_shape=tuple(jax.ShapeDtypeStruct(*shape) for shape in shapes),
        in_specs=[in_vmem] * 4,
        out_specs=(hbm,) * 4,
        scratch_shapes=[dma((4,))],
        compiler_params=pltpu.CompilerParams(vmem_limit_bytes=2**20),
    )(*results)
    return d_tokens, d_weight, d_gain.reshape(FEATS), d_log.reshape(ROWS)


def solution(mesh):
    in_specs = (
        P(("dp", "row"), "col"),
        P("col"),
        P("col", "row"),
        P(("dp", "col"), "row"),
        P(("dp", "row"), "col"),
    )
    out_specs = (P(("dp", "row"), "col"), P(("col", "dp"), "row"), P("col"), P(("dp", "row")))
    return jax.shard_map(local, mesh=mesh, in_specs=in_specs, out_specs=out_specs, check_vma=False)
```

```python
import jax
import jax.numpy as jnp
from jax import lax
from jax.experimental import pallas as pl
from jax.experimental.pallas import tpu as pltpu
from jax.sharding import PartitionSpec as P

MESH = pl.DeviceIdType.MESH
BF16, F32 = jnp.bfloat16, jnp.float32
D = 8192
TOKENS = 16384
ROWS = 512
FEATS = 2048
COLS = 1024
QUARTER = 256
SIDE = 4
SLABS = 8
CHUNKS = ((0, 1), (1, 1), (2, 2), (4, 2), (6, 2))
N = len(CHUNKS)
AHEAD = 3
LEAD = 1
STRAIGHT = ((0, 0), (0, 0), (0, 0), (0, 1), (1, 1))
ORDER = (
    ("M", 0), ("S", 0), ("M", 1), ("P", 0), ("S", 1), ("M", 2), ("P", 1), ("E", 0), ("S", 2), ("M", 3), ("P", 2), ("E", 1), ("Q", 0), ("S", 3), ("normed", 0), ("M", 4), ("S", 4), ("P", 3), ("normed", 1), ("inner", 0), ("E", 2), ("Q", 1), ("F", 0), ("E", 3), ("E", 4), ("Q", 2), ("F", 1), ("gain", 0), ("tokens", 0), ("F", 2), ("F", 3), ("F", 4),
)
PARTS = (((0, 4), (0, 4)), ((4, 8), (4, 8)))
FIRST_PEER = 0


def dot(a, b, dims):
    return lax.dot_general(a, b, ((dims[:1], dims[1:]), ((), ())), preferred_element_type=F32)


def kernel(*refs):
    it = iter(refs)
    tok_hbm, gain_hbm, w_hbm, dout_hbm, dres_hbm = [next(it) for _ in range(5)]
    dtok_ref, dw_ref, dgain_ref, dlog_ref = [next(it) for _ in range(4)]
    toks_both, grads, other, w, w_peer, dn, dres, scaled_t = [next(it) for _ in range(8)]
    tok, tok_peer = toks_both.at[pl.ds(0, ROWS)], toks_both.at[pl.ds(ROWS, ROWS)]
    gain_flat, gain_row, lanes, sq, inv_row, inv_col, coef_col, inner_buf = [next(it) for _ in range(8)]
    dg_acc, dg_a, dg_b, dw_t = [next(it) for _ in range(4)]
    part, got1a, got1b, mid, got2a, got2b = [[next(it) for _ in range(N)] for _ in range(6)]
    local_sem, ag_s, ag_r, tp_s, tp_r, wp_s, wp_r, ot_s, ot_r = [next(it) for _ in range(9)]
    sq_s, sq_r, in_s, in_r, ga_s, ga_r, gb_s, gb_r, rs_s, rs_r = [next(it) for _ in range(10)]

    dp, r, z = lax.axis_index("dp"), lax.axis_index("row"), lax.axis_index("col")
    y, x = dp // SIDE, dp % SIDE

    def dev(dy=0, dx=0, dr=0, dz=0):
        return ((y + dy) % SIDE * SIDE + (x + dx) % SIDE, (r + dr) % 2, (z + dz) % SIDE)

    def send(src, dst, ss, rs, to):
        pltpu.make_async_remote_copy(
            src_ref=src, dst_ref=dst, send_sem=ss, recv_sem=rs, device_id=to, device_id_type=MESH
        ).start()

    def descriptor(ref, sem):
        return pltpu.make_async_remote_copy(
            src_ref=ref, dst_ref=ref, send_sem=sem, recv_sem=sem, device_id=dev(dr=1), device_id_type=MESH
        )

    def arrived(ref, sem):
        descriptor(ref, sem).wait_recv()

    def left(ref, sem):
        descriptor(ref, sem).wait_send()

    def load(src, dst, i):
        c = pltpu.make_async_copy(src, dst, local_sem.at[i])
        c.start()
        return c

    def slot(q):
        return pl.ds(pl.multiple_of((q + 2 * r) % SIDE * QUARTER, QUARTER), QUARTER)

    def half_slot(q, half):
        return pl.ds(pl.multiple_of((q + 2 * r) % SIDE * QUARTER + half * 128, 128), 128)

    def slabs(k):
        return pl.ds(*CHUNKS[k])

    partners = [dev(dr=1)]
    partners += [dev(dz=d) for d in (1, 2, 3)] + [dev(dr=1, dz=d) for d in (1, 2, 3)]
    partners += [dev(dx=d) for d in (1, 2, 3)] + [dev(dr=1, dx=d) for d in (1, 2, 3)]
    partners += [dev(dy=d) for d in (1, 2, 3)]
    barrier = pltpu.get_barrier_semaphore()
    for partner in partners:
        pl.semaphore_signal(barrier, inc=1, device_id=partner, device_id_type=MESH)

    for c in range(SLABS):
        load(dout_hbm.at[:, pl.ds(c * 128, 128)], grads.at[c, slot(z)], 1)
    tok_load = load(tok_hbm, tok, 0)
    gain_load = load(gain_hbm, gain_flat, 2)
    w_load = load(w_hbm, w, 3)
    res_load = load(dres_hbm, dres, 4)

    def gather_send(c):
        own = grads.at[c, slot(z)]
        for d in (1, 3) if c else (1, 3, 2):
            send(own, own, ag_s, ag_r.at[c, 0], dev(dz=d))

    relayed = [0]

    def gather_relay(hi):
        while relayed[0] < min(hi, SLABS - 1):
            relayed[0] += 1
            c = relayed[0]
            arrived(grads.at[c, pl.ds(0, 2 * QUARTER)], ag_r.at[c, 0])
            low, high = grads.at[c, half_slot(z + 1, 0)], grads.at[c, half_slot(z + 3, 1)]
            send(low, low, ag_s, ag_r.at[c, 1], dev(dz=3))
            send(high, high, ag_s, ag_r.at[c, 1], dev(dz=1))
            if c + AHEAD < SLABS:
                gather_send(c + AHEAD)

    def gather_wait(k):
        for c in range(CHUNKS[k][0], sum(CHUNKS[k])):
            if c == 0:
                arrived(grads.at[c, pl.ds(0, 3 * QUARTER)], ag_r.at[c, 0])
            else:
                gather_relay(c + LEAD)
                arrived(grads.at[c, pl.ds(0, QUARTER)], ag_r.at[c, 1])
        send(grads.at[slabs(k), pl.ds(ROWS, ROWS)], other.at[slabs(k)], ot_s, ot_r.at[k], dev(dr=1))

    own_quarter = grads.at[:, slot(z)]
    pltpu.make_async_copy(own_quarter, own_quarter, local_sem.at[1]).wait()
    pl.semaphore_wait(barrier, len(partners))
    gather_send(0)
    for b in range(0, 2):
        cols = pl.ds(b * 512, 512)
        send(tok_hbm.at[:, cols], tok_peer.at[:, cols], tp_s, tp_r.at[b], dev(dr=1))

    tok_load.wait()

    @pl.loop(0, ROWS // 16)
    def _(i):
        rows = pl.ds(pl.multiple_of(i * 16, 16), 16)
        acc = jnp.zeros((16, 128), F32)
        for j in range(FEATS // 128):
            t = tok[rows, pl.ds(j * 128, 128)].astype(F32)
            acc += t * t
        lanes[rows, :] = acc

    def lane_sums():
        total = jnp.sum(lanes[...].T, axis=0, keepdims=True)
        return jnp.broadcast_to(total, (8, ROWS))

    own_sq = sq.at[z]
    own_sq[...] = lane_sums()
    peer_sq = sq.at[SIDE + z]
    for d in (1, 2, 3):
        send(own_sq, own_sq, sq_s, sq_r, dev(dz=d))
        send(own_sq, peer_sq, sq_s, sq_r, dev(dr=1, dz=d))
    send(own_sq, peer_sq, sq_s, sq_r, dev(dr=1))
    for c in range(1, AHEAD + 1):
        gather_send(c)
    for b in range(2, 4):
        cols = pl.ds(b * 512, 512)
        send(tok_hbm.at[:, cols], tok_peer.at[:, cols], tp_s, tp_r.at[b], dev(dr=1))
    send(w_hbm, w_peer, wp_s, wp_r, dev(dr=1))

    gain_load.wait()
    gain_row[...] = gain_flat[...].astype(F32).reshape(1, FEATS)

    arrived(sq.at[pl.ds(0, 7)], sq_r)
    for side in range(2):
        total = sq[4 * side] + sq[4 * side + 1] + sq[4 * side + 2] + sq[4 * side + 3]
        inv_row[:, pl.ds(side * ROWS, ROWS)] = lax.rsqrt(total * (1.0 / D) + 1e-05)

    def as_column(row):
        return jnp.broadcast_to(row[0:1], (128, ROWS)).T

    def product(k):
        first, count = CHUNKS[k]
        width, cq = count * 128, count * 32
        for c in range(count):
            for s in range(SIDE):
                toks = pl.ds(s * QUARTER, QUARTER)
                g = grads[first + c, toks, :].T.astype(F32)
                scaled_t[pl.ds(c * 128, 128), toks] = (g * inv_row[0:1, toks]).astype(BF16)

        def block(b):
            feats = pl.ds(b * 512, 512) if isinstance(b, int) else pl.ds(pl.multiple_of(b * 512, 512), 512)
            res = dot(scaled_t[pl.ds(0, width), :], toks_both[:, feats], (1, 0)).astype(BF16)
            for j in range(SIDE):
                for h in range(2):
                    for u in range(2):
                        lo = (2 * h + u) * cq
                        piece = res[lo : lo + cq, j * 128 : j * 128 + 128]
                        if h == 0:
                            part[k][h, j, u, b] = piece
                        else:
                            part[k][h, b, u, j] = piece

        if k == 0:
            for b in range(SIDE):
                arrived(tok_peer.at[:, pl.ds(b * 512, 512)], tp_r.at[b])
                block(b)
                if b > 0:
                    gather_relay(b)
        else:
            pl.loop(0, SIDE)(block)

    def axis(h, stage):
        if (h == 0) == (stage == 0):
            return x, (lambda d: dev(dx=d))
        return y, (lambda d: dev(dy=d))

    def buffers(stage):
        return (part, got1a, got1b) if stage == 0 else (mid, got2a, got2b)

    def reduce_start(k, stage):
        src, got_a, got_b = buffers(stage)
        ss, rs = rs_s.at[k, stage], rs_r.at[k, stage]
        for h in range(2):
            m, to = axis(h, stage)
            far, up, down = (m + 2) % SIDE, (m + 1) % SIDE, (m + 3) % SIDE
            if STRAIGHT[k][stage]:
                send(src[k].at[h, far], got_b[k].at[h, 1], ss, rs.at[0], to(2))
                send(src[k].at[h, up], got_b[k].at[h, 0], ss, rs.at[0], to(1))
                send(src[k].at[h, down], got_b[k].at[h, 2], ss, rs.at[0], to(3))
                continue
            send(src[k].at[h, far, 0], got_a[k].at[h, 0], ss, rs.at[1], to(1))
            send(src[k].at[h, far, 1], got_a[k].at[h, 1], ss, rs.at[1], to(3))
            send(src[k].at[h, up, 1], got_b[k].at[h, 0, 1], ss, rs.at[0], to(1))
            send(src[k].at[h, down, 0], got_b[k].at[h, 1, 0], ss, rs.at[0], to(3))

    def add(a, b):
        return (a.astype(F32) + b.astype(F32)).astype(BF16)

    def reduce_pass(k, stage):
        if STRAIGHT[k][stage]:
            return
        src, got_a, got_b = buffers(stage)
        ss, rs = rs_s.at[k, stage], rs_r.at[k, stage]
        arrived(got_a[k], rs.at[1])
        for h in range(2):
            m, to = axis(h, stage)
            up, down = (m + 1) % SIDE, (m + 3) % SIDE
            src[k][h, up, 0] = add(src[k][h, up, 0], got_a[k][h, 0])
            send(src[k].at[h, up, 0], got_b[k].at[h, 0, 0], ss, rs.at[0], to(1))
            src[k][h, down, 1] = add(src[k][h, down, 1], got_a[k][h, 1])
            send(src[k].at[h, down, 1], got_b[k].at[h, 1, 1], ss, rs.at[0], to(3))

    def reduce_end(k, stage):
        src, _, got_b = buffers(stage)
        cq = CHUNKS[k][1] * 32
        arrived(got_b[k], rs_r.at[k, stage, 0])
        for h in range(2):
            m, _ = axis(h, stage)
            for u in range(2):
                total = src[k][h, m, u].astype(F32)
                for d in range(3 if STRAIGHT[k][stage] else 2):
                    total += got_b[k][h, d, u].astype(F32)
                if stage == 0:
                    for t in range(SIDE):
                        mid[k][h, t, u] = total[t].astype(BF16)
                else:
                    dw_t[pl.ds((2 * h + u) * cq, cq), :] = total

    def finish(k):
        first, count = CHUNKS[k]
        own = gain_row[0:1, pl.ds(pl.multiple_of(dp * 128, 128), 128)] * float(TOKENS) ** (-0.5)
        dw_ref[:, pl.ds(first * 128, count * 128)] = (dw_t[pl.ds(0, count * 128), :] * own).T.astype(BF16)

    def normed_grad(p):
        sources = [(grads, w, PARTS[p][0]), (other, w_peer, PARTS[p][1])]
        if PARTS[p][1]:
            for k in range(N):
                if CHUNKS[k][0] in range(*PARTS[p][1]):
                    arrived(other.at[slabs(k)], ot_r.at[k])
        if p == 0:
            w_load.wait()
        if p == FIRST_PEER:
            arrived(w_peer, wp_r)

        @pl.loop(0, SIDE)
        def _(b):
            feats = pl.ds(pl.multiple_of(b * 512, 512), 512)
            rows, weights = [], []
            for grad, weight, span in sources:
                if span:
                    rows += [grad[c, pl.ds(0, ROWS), :] for c in range(*span)]
                    weights.append(weight[feats, pl.ds(span[0] * 128, (span[1] - span[0]) * 128)])
            res = dot(jnp.concatenate(rows, axis=1), jnp.concatenate(weights, axis=1), (1, 1))
            if p == 0:
                dn[:, feats] = res
            else:
                dn[:, feats] += res

    def inner_start():
        inv_col[...] = as_column(inv_row[:, 0:ROWS])
        dg_acc[...] = jnp.zeros_like(dg_acc)

        @pl.loop(0, ROWS // 16)
        def _(i):
            rows = pl.ds(pl.multiple_of(i * 16, 16), 16)
            inv = inv_col[rows, :]
            acc = jnp.zeros((16, 128), F32)
            for j in range(FEATS // 128):
                cols = pl.ds(j * 128, 128)
                prod = dn[rows, cols] * tok[rows, cols].astype(F32)
                acc += prod * gain_row[0:1, cols]
                prod = prod * inv
                dg_acc[:, cols] += prod[0:8] + prod[8:16]
            lanes[rows, :] = acc

        own_inner = inner_buf.at[z]
        own_inner[...] = lane_sums()
        for d in (1, 2, 3):
            send(own_inner, own_inner, in_s, in_r, dev(dz=d))
        own_dg = dg_a.at[r * SIDE + x]
        for j in range(FEATS // 128):
            own_dg[pl.ds(j, 1), :] = jnp.sum(dg_acc[:, pl.ds(j * 128, 128)], axis=0, keepdims=True)
        for d in (1, 2, 3):
            send(own_dg, own_dg, ga_s, ga_r, dev(dx=d))
            send(own_dg, own_dg, ga_s, ga_r, dev(dr=1, dx=d))
        send(own_dg, own_dg, ga_s, ga_r, dev(dr=1))

    def gain_y():
        arrived(dg_a.at[pl.ds(0, 7)], ga_r)
        total = dg_a[0]
        for i in range(1, 8):
            total += dg_a[i]
        own_dg = dg_b.at[y]
        own_dg[...] = total
        for d in (1, 2, 3):
            send(own_dg, own_dg, gb_s, gb_r, dev(dy=d))

    def gain_end():
        arrived(dg_b.at[pl.ds(0, 3)], gb_r)
        dgain_ref[...] = (dg_b[0] + dg_b[1] + dg_b[2] + dg_b[3]) * float(TOKENS) ** (-0.5)

    def tokens_end():
        arrived(inner_buf.at[pl.ds(0, 3)], in_r)
        inner = inner_buf[0] + inner_buf[1] + inner_buf[2] + inner_buf[3]
        inv = inv_row[:, 0:ROWS]
        log_scale = inner * inv * float(D) ** (-0.5)
        for j in range(SIDE):
            dlog_ref[pl.ds(j, 1), :] = log_scale[0:1, j * 128 : j * 128 + 128]
        coef_col[...] = as_column(inv * inv * inv * inner * (1.0 / D))
        res_load.wait()

        @pl.loop(0, ROWS // 16)
        def _(i):
            rows = pl.ds(pl.multiple_of(i * 16, 16), 16)
            inv_c, coef = inv_col[rows, :], coef_col[rows, :]
            for j in range(FEATS // 128):
                cols = pl.ds(j * 128, 128)
                scaled = dn[rows, cols] * gain_row[0:1, cols]
                value = dres[rows, cols].astype(F32) + inv_c * scaled
                dtok_ref[rows, cols] = (value - tok[rows, cols].astype(F32) * coef).astype(BF16)

    def step(k, n):
        if n == 0:
            gather_wait(k)
            product(k)
            gather_relay(sum(CHUNKS[k]) + LEAD)
        if n == 5:
            reduce_start(k, 0)
        if n == 1:
            reduce_pass(k, 0)
        if n == 2:
            reduce_end(k, 0)
            reduce_start(k, 1)
        if n == 3:
            reduce_pass(k, 1)
        if n == 4:
            reduce_end(k, 1)
            finish(k)

    for what, k in ORDER:
        if what == "normed":
            normed_grad(k)
        elif what == "inner":
            inner_start()
        elif what == "tokens":
            tokens_end()
        elif what == "gain":
            gain_y()
        else:
            step(k, "MPEQFS".index(what))
    gain_end()
    left(grads.at[pl.ds(0, 6)], ag_s)
    left(tok_peer, tp_s)
    left(w_peer, wp_s)
    left(other, ot_s)
    left(sq.at[pl.ds(0, 7)], sq_s)
    left(inner_buf.at[pl.ds(0, 3)], in_s)
    left(dg_a.at[pl.ds(0, 7)], ga_s)
    left(dg_b.at[pl.ds(0, 3)], gb_s)
    for k in range(N):
        left(part[k].at[:, pl.ds(0, 3)], rs_s.at[k, 0])
        left(mid[k].at[:, pl.ds(0, 3)], rs_s.at[k, 1])


def write_out(dtok, dw, dgain, dlog, dtok_hbm, dw_hbm, dgain_hbm, dlog_hbm, sem):
    pairs = ((dtok, dtok_hbm), (dw, dw_hbm), (dgain, dgain_hbm), (dlog, dlog_hbm))
    copies = [pltpu.make_async_copy(src, dst, sem.at[i]) for i, (src, dst) in enumerate(pairs)]
    for c in copies:
        c.start()
    for c in copies:
        c.wait()


def local(tokens, gain, weight, d_out, d_residual):
    vmem, dma = pltpu.VMEM, pltpu.SemaphoreType.DMA
    cqs = [count * 32 for _, count in CHUNKS]
    scratch = [
        vmem((2 * ROWS, FEATS), BF16),
        vmem((SLABS, 2 * ROWS, 128), BF16),
        vmem((SLABS, ROWS, 128), BF16),
        vmem((FEATS, COLS), BF16),
        vmem((FEATS, COLS), BF16),
        vmem((ROWS, FEATS), F32),
        vmem((ROWS, FEATS), BF16),
        vmem((256, 2 * ROWS), BF16),
        vmem((FEATS,), BF16),
        vmem((1, FEATS), F32),
        vmem((ROWS, 128), F32),
        vmem((2 * SIDE, 8, ROWS), F32),
        vmem((8, 2 * ROWS), F32),
        vmem((ROWS, 128), F32),
        vmem((ROWS, 128), F32),
        vmem((SIDE, 8, ROWS), F32),
        vmem((8, FEATS), F32),
        vmem((2 * SIDE, 16, 128), F32),
        vmem((SIDE, 16, 128), F32),
        vmem((256, 128), F32),
    ]
    scratch += [vmem((2, SIDE, 2, SIDE, c, 128), BF16) for c in cqs]
    scratch += [vmem((2, 2, SIDE, c, 128), BF16) for c in cqs]
    scratch += [vmem((2, 2 + s[0], 2, SIDE, c, 128), BF16) for c, s in zip(cqs, STRAIGHT)]
    scratch += [vmem((2, SIDE, 2, c, 128), BF16) for c in cqs]
    scratch += [vmem((2, 2, c, 128), BF16) for c in cqs]
    scratch += [vmem((2, 2 + s[1], 2, c, 128), BF16) for c, s in zip(cqs, STRAIGHT)]
    scratch += [
        dma((5,)),
        dma,
        dma((SLABS, 2)),
        dma,
        dma((SIDE,)),
        dma,
        dma,
        dma,
        dma((N,)),
        dma,
        dma,
        dma,
        dma,
        dma,
        dma,
        dma,
        dma,
        dma((N, 2)),
        dma((N, 2, 2)),
    ]
    hbm, in_vmem = pl.BlockSpec(memory_space=pltpu.HBM), pl.BlockSpec(memory_space=pltpu.VMEM)
    shapes = (((ROWS, FEATS), BF16), ((128, COLS), BF16), ((16, 128), F32), ((4, 128), F32))
    results = pl.pallas_call(
        kernel,
        name="fused",
        out_shape=tuple(pltpu.VMEM(*shape) for shape in shapes),
        in_specs=[hbm] * 5,
        out_specs=(in_vmem,) * 4,
        scratch_shapes=scratch,
        compiler_params=pltpu.CompilerParams(
            collective_id=0, has_side_effects=True, vmem_limit_bytes=48 * 2**20
        ),
        cost_estimate=pl.CostEstimate(flops=8 * 2**30, bytes_accessed=12 * 2**20, transcendentals=0),
    )(*[pltpu.with_memory_space_constraint(a, pltpu.HBM) for a in (tokens, gain, weight, d_out, d_residual)])
    d_tokens, d_weight, d_gain, d_log = pl.pallas_call(
        write_out,
        name="write_out",
        out_shape=tuple(jax.ShapeDtypeStruct(*shape) for shape in shapes),
        in_specs=[in_vmem] * 4,
        out_specs=(hbm,) * 4,
        scratch_shapes=[dma((4,))],
        compiler_params=pltpu.CompilerParams(vmem_limit_bytes=2**20),
    )(*results)
    return d_tokens, d_weight, d_gain.reshape(FEATS), d_log.reshape(ROWS)


def solution(mesh):
    in_specs = (
        P(("dp", "row"), "col"),
        P("col"),
        P("col", "row"),
        P(("dp", "col"), "row"),
        P(("dp", "row"), "col"),
    )
    out_specs = (P(("dp", "row"), "col"), P(("col", "dp"), "row"), P("col"), P(("dp", "row")))
    return jax.shard_map(local, mesh=mesh, in_specs=in_specs, out_specs=out_specs, check_vma=False)
```

```python
import jax
import jax.numpy as jnp
from jax import lax
from jax.experimental import pallas as pl
from jax.experimental.pallas import tpu as pltpu
from jax.sharding import PartitionSpec as P

MESH = pl.DeviceIdType.MESH
BF16, F32 = jnp.bfloat16, jnp.float32
D = 8192
TOKENS = 16384
ROWS = 512
FEATS = 2048
COLS = 1024
QUARTER = 256
SIDE = 4
SLABS = 8
CHUNKS = ((0, 1), (1, 1), (2, 2), (4, 2), (6, 2))
N = len(CHUNKS)
AHEAD = 3
LEAD = 2
STRAIGHT = ((0, 0), (0, 0), (0, 0), (0, 1), (1, 1))
ORDER = (
    ("M", 0), ("S", 0), ("M", 1), ("P", 0), ("S", 1), ("M", 2), ("P", 1), ("E", 0), ("S", 2), ("M", 3), ("P", 2), ("E", 1), ("Q", 0), ("S", 3), ("normed", 0), ("M", 4), ("S", 4), ("P", 3), ("normed", 1), ("inner", 0), ("E", 2), ("Q", 1), ("F", 0), ("E", 3), ("E", 4), ("Q", 2), ("F", 1), ("gain", 0), ("tokens", 0), ("F", 2), ("F", 3), ("F", 4),
)
PARTS = (((0, 4), (0, 4)), ((4, 8), (4, 8)))
FIRST_PEER = 0


def dot(a, b, dims):
    return lax.dot_general(a, b, ((dims[:1], dims[1:]), ((), ())), preferred_element_type=F32)


def kernel(*refs):
    it = iter(refs)
    tok_hbm, gain_hbm, w_hbm, dout_hbm, dres_hbm = [next(it) for _ in range(5)]
    dtok_ref, dw_ref, dgain_ref, dlog_ref = [next(it) for _ in range(4)]
    toks_both, grads, other, w, w_peer, dn, dres, scaled_t = [next(it) for _ in range(8)]
    tok, tok_peer = toks_both.at[pl.ds(0, ROWS)], toks_both.at[pl.ds(ROWS, ROWS)]
    gain_flat, gain_row, lanes, sq, inv_row, inv_col, coef_col, inner_buf = [next(it) for _ in range(8)]
    dg_acc, dg_a, dg_b, dw_t = [next(it) for _ in range(4)]
    part, got1a, got1b, mid, got2a, got2b = [[next(it) for _ in range(N)] for _ in range(6)]
    local_sem, ag_s, ag_r, tp_s, tp_r, wp_s, wp_r, ot_s, ot_r = [next(it) for _ in range(9)]
    sq_s, sq_r, in_s, in_r, ga_s, ga_r, gb_s, gb_r, rs_s, rs_r = [next(it) for _ in range(10)]

    dp, r, z = lax.axis_index("dp"), lax.axis_index("row"), lax.axis_index("col")
    y, x = dp // SIDE, dp % SIDE

    def dev(dy=0, dx=0, dr=0, dz=0):
        return ((y + dy) % SIDE * SIDE + (x + dx) % SIDE, (r + dr) % 2, (z + dz) % SIDE)

    def send(src, dst, ss, rs, to):
        pltpu.make_async_remote_copy(
            src_ref=src, dst_ref=dst, send_sem=ss, recv_sem=rs, device_id=to, device_id_type=MESH
        ).start()

    def descriptor(ref, sem):
        return pltpu.make_async_remote_copy(
            src_ref=ref, dst_ref=ref, send_sem=sem, recv_sem=sem, device_id=dev(dr=1), device_id_type=MESH
        )

    def arrived(ref, sem):
        descriptor(ref, sem).wait_recv()

    def left(ref, sem):
        descriptor(ref, sem).wait_send()

    def load(src, dst, i):
        c = pltpu.make_async_copy(src, dst, local_sem.at[i])
        c.start()
        return c

    def slot(q):
        return pl.ds(pl.multiple_of((q + 2 * r) % SIDE * QUARTER, QUARTER), QUARTER)

    def half_slot(q, half):
        return pl.ds(pl.multiple_of((q + 2 * r) % SIDE * QUARTER + half * 128, 128), 128)

    def slabs(k):
        return pl.ds(*CHUNKS[k])

    partners = [dev(dr=1)]
    partners += [dev(dz=d) for d in (1, 2, 3)] + [dev(dr=1, dz=d) for d in (1, 2, 3)]
    partners += [dev(dx=d) for d in (1, 2, 3)] + [dev(dr=1, dx=d) for d in (1, 2, 3)]
    partners += [dev(dy=d) for d in (1, 2, 3)]
    barrier = pltpu.get_barrier_semaphore()
    for partner in partners:
        pl.semaphore_signal(barrier, inc=1, device_id=partner, device_id_type=MESH)

    for c in range(SLABS):
        load(dout_hbm.at[:, pl.ds(c * 128, 128)], grads.at[c, slot(z)], 1)
    tok_load = load(tok_hbm, tok, 0)
    gain_load = load(gain_hbm, gain_flat, 2)
    w_load = load(w_hbm, w, 3)
    res_load = load(dres_hbm, dres, 4)

    def gather_send(c):
        own = grads.at[c, slot(z)]
        for d in (1, 3) if c else (1, 3, 2):
            send(own, own, ag_s, ag_r.at[c, 0], dev(dz=d))

    relayed = [0]

    def gather_relay(hi):
        while relayed[0] < min(hi, SLABS - 1):
            relayed[0] += 1
            c = relayed[0]
            arrived(grads.at[c, pl.ds(0, 2 * QUARTER)], ag_r.at[c, 0])
            low, high = grads.at[c, half_slot(z + 1, 0)], grads.at[c, half_slot(z + 3, 1)]
            send(low, low, ag_s, ag_r.at[c, 1], dev(dz=3))
            send(high, high, ag_s, ag_r.at[c, 1], dev(dz=1))
            if c + AHEAD < SLABS:
                gather_send(c + AHEAD)

    def gather_wait(k):
        for c in range(CHUNKS[k][0], sum(CHUNKS[k])):
            if c == 0:
                arrived(grads.at[c, pl.ds(0, 3 * QUARTER)], ag_r.at[c, 0])
            else:
                gather_relay(c + LEAD)
                arrived(grads.at[c, pl.ds(0, QUARTER)], ag_r.at[c, 1])
        send(grads.at[slabs(k), pl.ds(ROWS, ROWS)], other.at[slabs(k)], ot_s, ot_r.at[k], dev(dr=1))

    own_quarter = grads.at[:, slot(z)]
    pltpu.make_async_copy(own_quarter, own_quarter, local_sem.at[1]).wait()
    pl.semaphore_wait(barrier, len(partners))
    gather_send(0)
    for b in range(0, 2):
        cols = pl.ds(b * 512, 512)
        send(tok_hbm.at[:, cols], tok_peer.at[:, cols], tp_s, tp_r.at[b], dev(dr=1))

    tok_load.wait()

    @pl.loop(0, ROWS // 16)
    def _(i):
        rows = pl.ds(pl.multiple_of(i * 16, 16), 16)
        acc = jnp.zeros((16, 128), F32)
        for j in range(FEATS // 128):
            t = tok[rows, pl.ds(j * 128, 128)].astype(F32)
            acc += t * t
        lanes[rows, :] = acc

    def lane_sums():
        total = jnp.sum(lanes[...].T, axis=0, keepdims=True)
        return jnp.broadcast_to(total, (8, ROWS))

    own_sq = sq.at[z]
    own_sq[...] = lane_sums()
    peer_sq = sq.at[SIDE + z]
    for d in (1, 2, 3):
        send(own_sq, own_sq, sq_s, sq_r, dev(dz=d))
        send(own_sq, peer_sq, sq_s, sq_r, dev(dr=1, dz=d))
    send(own_sq, peer_sq, sq_s, sq_r, dev(dr=1))
    for c in range(1, AHEAD + 1):
        gather_send(c)
    for b in range(2, 4):
        cols = pl.ds(b * 512, 512)
        send(tok_hbm.at[:, cols], tok_peer.at[:, cols], tp_s, tp_r.at[b], dev(dr=1))
    send(w_hbm, w_peer, wp_s, wp_r, dev(dr=1))

    gain_load.wait()
    gain_row[...] = gain_flat[...].astype(F32).reshape(1, FEATS)

    arrived(sq.at[pl.ds(0, 7)], sq_r)
    for side in range(2):
        total = sq[4 * side] + sq[4 * side + 1] + sq[4 * side + 2] + sq[4 * side + 3]
        inv_row[:, pl.ds(side * ROWS, ROWS)] = lax.rsqrt(total * (1.0 / D) + 1e-05)

    def as_column(row):
        return jnp.broadcast_to(row[0:1], (128, ROWS)).T

    def product(k):
        first, count = CHUNKS[k]
        width, cq = count * 128, count * 32
        for c in range(count):
            for s in range(SIDE):
                toks = pl.ds(s * QUARTER, QUARTER)
                g = grads[first + c, toks, :].T.astype(F32)
                scaled_t[pl.ds(c * 128, 128), toks] = (g * inv_row[0:1, toks]).astype(BF16)

        def block(b):
            feats = pl.ds(b * 512, 512) if isinstance(b, int) else pl.ds(pl.multiple_of(b * 512, 512), 512)
            res = dot(scaled_t[pl.ds(0, width), :], toks_both[:, feats], (1, 0)).astype(BF16)
            for j in range(SIDE):
                for h in range(2):
                    for u in range(2):
                        lo = (2 * h + u) * cq
                        piece = res[lo : lo + cq, j * 128 : j * 128 + 128]
                        if h == 0:
                            part[k][h, j, u, b] = piece
                        else:
                            part[k][h, b, u, j] = piece

        if k == 0:
            for b in range(SIDE):
                arrived(tok_peer.at[:, pl.ds(b * 512, 512)], tp_r.at[b])
                block(b)
                if b > 0:
                    gather_relay(b)
        else:
            pl.loop(0, SIDE)(block)

    def axis(h, stage):
        if (h == 0) == (stage == 0):
            return x, (lambda d: dev(dx=d))
        return y, (lambda d: dev(dy=d))

    def buffers(stage):
        return (part, got1a, got1b) if stage == 0 else (mid, got2a, got2b)

    def reduce_start(k, stage):
        src, got_a, got_b = buffers(stage)
        ss, rs = rs_s.at[k, stage], rs_r.at[k, stage]
        for h in range(2):
            m, to = axis(h, stage)
            far, up, down = (m + 2) % SIDE, (m + 1) % SIDE, (m + 3) % SIDE
            if STRAIGHT[k][stage]:
                send(src[k].at[h, far], got_b[k].at[h, 1], ss, rs.at[0], to(2))
                send(src[k].at[h, up], got_b[k].at[h, 0], ss, rs.at[0], to(1))
                send(src[k].at[h, down], got_b[k].at[h, 2], ss, rs.at[0], to(3))
                continue
            send(src[k].at[h, far, 0], got_a[k].at[h, 0], ss, rs.at[1], to(1))
            send(src[k].at[h, far, 1], got_a[k].at[h, 1], ss, rs.at[1], to(3))
            send(src[k].at[h, up, 1], got_b[k].at[h, 0, 1], ss, rs.at[0], to(1))
            send(src[k].at[h, down, 0], got_b[k].at[h, 1, 0], ss, rs.at[0], to(3))

    def add(a, b):
        return (a.astype(F32) + b.astype(F32)).astype(BF16)

    def reduce_pass(k, stage):
        if STRAIGHT[k][stage]:
            return
        src, got_a, got_b = buffers(stage)
        ss, rs = rs_s.at[k, stage], rs_r.at[k, stage]
        arrived(got_a[k], rs.at[1])
        for h in range(2):
            m, to = axis(h, stage)
            up, down = (m + 1) % SIDE, (m + 3) % SIDE
            src[k][h, up, 0] = add(src[k][h, up, 0], got_a[k][h, 0])
            send(src[k].at[h, up, 0], got_b[k].at[h, 0, 0], ss, rs.at[0], to(1))
            src[k][h, down, 1] = add(src[k][h, down, 1], got_a[k][h, 1])
            send(src[k].at[h, down, 1], got_b[k].at[h, 1, 1], ss, rs.at[0], to(3))

    def reduce_end(k, stage):
        src, _, got_b = buffers(stage)
        cq = CHUNKS[k][1] * 32
        arrived(got_b[k], rs_r.at[k, stage, 0])
        for h in range(2):
            m, _ = axis(h, stage)
            for u in range(2):
                total = src[k][h, m, u].astype(F32)
                for d in range(3 if STRAIGHT[k][stage] else 2):
                    total += got_b[k][h, d, u].astype(F32)
                if stage == 0:
                    for t in range(SIDE):
                        mid[k][h, t, u] = total[t].astype(BF16)
                else:
                    dw_t[pl.ds((2 * h + u) * cq, cq), :] = total

    def finish(k):
        first, count = CHUNKS[k]
        own = gain_row[0:1, pl.ds(pl.multiple_of(dp * 128, 128), 128)] * float(TOKENS) ** (-0.5)
        dw_ref[:, pl.ds(first * 128, count * 128)] = (dw_t[pl.ds(0, count * 128), :] * own).T.astype(BF16)

    def normed_grad(p):
        sources = [(grads, w, PARTS[p][0]), (other, w_peer, PARTS[p][1])]
        if PARTS[p][1]:
            for k in range(N):
                if CHUNKS[k][0] in range(*PARTS[p][1]):
                    arrived(other.at[slabs(k)], ot_r.at[k])
        if p == 0:
            w_load.wait()
        if p == FIRST_PEER:
            arrived(w_peer, wp_r)

        @pl.loop(0, SIDE)
        def _(b):
            feats = pl.ds(pl.multiple_of(b * 512, 512), 512)
            rows, weights = [], []
            for grad, weight, span in sources:
                if span:
                    rows += [grad[c, pl.ds(0, ROWS), :] for c in range(*span)]
                    weights.append(weight[feats, pl.ds(span[0] * 128, (span[1] - span[0]) * 128)])
            res = dot(jnp.concatenate(rows, axis=1), jnp.concatenate(weights, axis=1), (1, 1))
            if p == 0:
                dn[:, feats] = res
            else:
                dn[:, feats] += res

    def inner_start():
        inv_col[...] = as_column(inv_row[:, 0:ROWS])
        dg_acc[...] = jnp.zeros_like(dg_acc)

        @pl.loop(0, ROWS // 16)
        def _(i):
            rows = pl.ds(pl.multiple_of(i * 16, 16), 16)
            inv = inv_col[rows, :]
            acc = jnp.zeros((16, 128), F32)
            for j in range(FEATS // 128):
                cols = pl.ds(j * 128, 128)
                prod = dn[rows, cols] * tok[rows, cols].astype(F32)
                acc += prod * gain_row[0:1, cols]
                prod = prod * inv
                dg_acc[:, cols] += prod[0:8] + prod[8:16]
            lanes[rows, :] = acc

        own_inner = inner_buf.at[z]
        own_inner[...] = lane_sums()
        for d in (1, 2, 3):
            send(own_inner, own_inner, in_s, in_r, dev(dz=d))
        own_dg = dg_a.at[r * SIDE + x]
        for j in range(FEATS // 128):
            own_dg[pl.ds(j, 1), :] = jnp.sum(dg_acc[:, pl.ds(j * 128, 128)], axis=0, keepdims=True)
        for d in (1, 2, 3):
            send(own_dg, own_dg, ga_s, ga_r, dev(dx=d))
            send(own_dg, own_dg, ga_s, ga_r, dev(dr=1, dx=d))
        send(own_dg, own_dg, ga_s, ga_r, dev(dr=1))

    def gain_y():
        arrived(dg_a.at[pl.ds(0, 7)], ga_r)
        total = dg_a[0]
        for i in range(1, 8):
            total += dg_a[i]
        own_dg = dg_b.at[y]
        own_dg[...] = total
        for d in (1, 2, 3):
            send(own_dg, own_dg, gb_s, gb_r, dev(dy=d))

    def gain_end():
        arrived(dg_b.at[pl.ds(0, 3)], gb_r)
        dgain_ref[...] = (dg_b[0] + dg_b[1] + dg_b[2] + dg_b[3]) * float(TOKENS) ** (-0.5)

    def tokens_end():
        arrived(inner_buf.at[pl.ds(0, 3)], in_r)
        inner = inner_buf[0] + inner_buf[1] + inner_buf[2] + inner_buf[3]
        inv = inv_row[:, 0:ROWS]
        log_scale = inner * inv * float(D) ** (-0.5)
        for j in range(SIDE):
            dlog_ref[pl.ds(j, 1), :] = log_scale[0:1, j * 128 : j * 128 + 128]
        coef_col[...] = as_column(inv * inv * inv * inner * (1.0 / D))
        res_load.wait()

        @pl.loop(0, ROWS // 16)
        def _(i):
            rows = pl.ds(pl.multiple_of(i * 16, 16), 16)
            inv_c, coef = inv_col[rows, :], coef_col[rows, :]
            for j in range(FEATS // 128):
                cols = pl.ds(j * 128, 128)
                scaled = dn[rows, cols] * gain_row[0:1, cols]
                value = dres[rows, cols].astype(F32) + inv_c * scaled
                dtok_ref[rows, cols] = (value - tok[rows, cols].astype(F32) * coef).astype(BF16)

    def step(k, n):
        if n == 0:
            gather_wait(k)
            product(k)
            gather_relay(sum(CHUNKS[k]) + LEAD)
        if n == 5:
            reduce_start(k, 0)
        if n == 1:
            reduce_pass(k, 0)
        if n == 2:
            reduce_end(k, 0)
            reduce_start(k, 1)
        if n == 3:
            reduce_pass(k, 1)
        if n == 4:
            reduce_end(k, 1)
            finish(k)

    for what, k in ORDER:
        if what == "normed":
            normed_grad(k)
        elif what == "inner":
            inner_start()
        elif what == "tokens":
            tokens_end()
        elif what == "gain":
            gain_y()
        else:
            step(k, "MPEQFS".index(what))
    gain_end()
    left(grads.at[pl.ds(0, 6)], ag_s)
    left(tok_peer, tp_s)
    left(w_peer, wp_s)
    left(other, ot_s)
    left(sq.at[pl.ds(0, 7)], sq_s)
    left(inner_buf.at[pl.ds(0, 3)], in_s)
    left(dg_a.at[pl.ds(0, 7)], ga_s)
    left(dg_b.at[pl.ds(0, 3)], gb_s)
    for k in range(N):
        left(part[k].at[:, pl.ds(0, 3)], rs_s.at[k, 0])
        left(mid[k].at[:, pl.ds(0, 3)], rs_s.at[k, 1])


def write_out(dtok, dw, dgain, dlog, dtok_hbm, dw_hbm, dgain_hbm, dlog_hbm, sem):
    pairs = ((dtok, dtok_hbm), (dw, dw_hbm), (dgain, dgain_hbm), (dlog, dlog_hbm))
    copies = [pltpu.make_async_copy(src, dst, sem.at[i]) for i, (src, dst) in enumerate(pairs)]
    for c in copies:
        c.start()
    for c in copies:
        c.wait()


def local(tokens, gain, weight, d_out, d_residual):
    vmem, dma = pltpu.VMEM, pltpu.SemaphoreType.DMA
    cqs = [count * 32 for _, count in CHUNKS]
    scratch = [
        vmem((2 * ROWS, FEATS), BF16),
        vmem((SLABS, 2 * ROWS, 128), BF16),
        vmem((SLABS, ROWS, 128), BF16),
        vmem((FEATS, COLS), BF16),
        vmem((FEATS, COLS), BF16),
        vmem((ROWS, FEATS), F32),
        vmem((ROWS, FEATS), BF16),
        vmem((256, 2 * ROWS), BF16),
        vmem((FEATS,), BF16),
        vmem((1, FEATS), F32),
        vmem((ROWS, 128), F32),
        vmem((2 * SIDE, 8, ROWS), F32),
        vmem((8, 2 * ROWS), F32),
        vmem((ROWS, 128), F32),
        vmem((ROWS, 128), F32),
        vmem((SIDE, 8, ROWS), F32),
        vmem((8, FEATS), F32),
        vmem((2 * SIDE, 16, 128), F32),
        vmem((SIDE, 16, 128), F32),
        vmem((256, 128), F32),
    ]
    scratch += [vmem((2, SIDE, 2, SIDE, c, 128), BF16) for c in cqs]
    scratch += [vmem((2, 2, SIDE, c, 128), BF16) for c in cqs]
    scratch += [vmem((2, 2 + s[0], 2, SIDE, c, 128), BF16) for c, s in zip(cqs, STRAIGHT)]
    scratch += [vmem((2, SIDE, 2, c, 128), BF16) for c in cqs]
    scratch += [vmem((2, 2, c, 128), BF16) for c in cqs]
    scratch += [vmem((2, 2 + s[1], 2, c, 128), BF16) for c, s in zip(cqs, STRAIGHT)]
    scratch += [
        dma((5,)),
        dma,
        dma((SLABS, 2)),
        dma,
        dma((SIDE,)),
        dma,
        dma,
        dma,
        dma((N,)),
        dma,
        dma,
        dma,
        dma,
        dma,
        dma,
        dma,
        dma,
        dma((N, 2)),
        dma((N, 2, 2)),
    ]
    hbm, in_vmem = pl.BlockSpec(memory_space=pltpu.HBM), pl.BlockSpec(memory_space=pltpu.VMEM)
    shapes = (((ROWS, FEATS), BF16), ((128, COLS), BF16), ((16, 128), F32), ((4, 128), F32))
    results = pl.pallas_call(
        kernel,
        name="fused",
        out_shape=tuple(pltpu.VMEM(*shape) for shape in shapes),
        in_specs=[hbm] * 5,
        out_specs=(in_vmem,) * 4,
        scratch_shapes=scratch,
        compiler_params=pltpu.CompilerParams(
            collective_id=0, has_side_effects=True, vmem_limit_bytes=48 * 2**20
        ),
        cost_estimate=pl.CostEstimate(flops=8 * 2**30, bytes_accessed=12 * 2**20, transcendentals=0),
    )(*[pltpu.with_memory_space_constraint(a, pltpu.HBM) for a in (tokens, gain, weight, d_out, d_residual)])
    d_tokens, d_weight, d_gain, d_log = pl.pallas_call(
        write_out,
        name="write_out",
        out_shape=tuple(jax.ShapeDtypeStruct(*shape) for shape in shapes),
        in_specs=[in_vmem] * 4,
        out_specs=(hbm,) * 4,
        scratch_shapes=[dma((4,))],
        compiler_params=pltpu.CompilerParams(vmem_limit_bytes=2**20),
    )(*results)
    return d_tokens, d_weight, d_gain.reshape(FEATS), d_log.reshape(ROWS)


def solution(mesh):
    in_specs = (
        P(("dp", "row"), "col"),
        P("col"),
        P("col", "row"),
        P(("dp", "col"), "row"),
        P(("dp", "row"), "col"),
    )
    out_specs = (P(("dp", "row"), "col"), P(("col", "dp"), "row"), P("col"), P(("dp", "row")))
    return jax.shard_map(local, mesh=mesh, in_specs=in_specs, out_specs=out_specs, check_vma=False)
```
